32 devices in a mesh: blk: 8 (over z, y), pb: 4 (over x, core).
Axes of the slice: x: 2, y: 2, z: 4, core: 2. Of those that a mesh axis runs over, the one named last changes fastest.
Arguments:
- query_rows: bfloat16 [10240, 1024], P(('blk', 'pb')), may hold values from -64 to 64
- key_rows: bfloat16 [10240, 1024], P(('blk', 'pb')), may hold values from -64 to 64
- partner: int32 [8, 1280], P('blk', 'pb'), may hold values from 0 to 1279, each once within a row
Outputs:
- pair_loss: float32 [10240], P(('blk', 'pb'))
- grad_queries: float32 [10240, 1024], P(('blk', 'pb'))
- grad_keys: float32 [10240, 1024], P(('blk', 'pb'))
The draws below stay inside these ranges and needn't reach their ends.
Inputs may be any that keep to these rules, and one draw needn't show every extreme that they name: Each row of partner is a permutation of 0 .. 1279.
All inputs are finite; a program needn't handle non-finite values.
Results may differ from the reference program's by a relative error of at most 0.0015.
Values may be sent and summed in bfloat16 or wider, within the bound.
No kernel may reach another device: no remote copies, remote signals or barrier semaphores. Data moves between devices by JAX's collectives and lax.ppermute only.
A program may use at most 192 MiB of HBM per device.

```python
import math
import jax
import jax.numpy as jnp
from jax import lax

D = 1024
WIN = 4
BLK = 1280
BLOCKS = 8
ROWS = 10240


def draw_pair(key):
    base = jax.random.fold_in(key, 4099)
    streams = jax.random.split(base, 5)
    shape = (ROWS, D)
    query_base = jax.random.normal(streams[0], shape, jnp.float32)
    key_base = jax.random.normal(streams[1], shape, jnp.float32)
    query_scale = jnp.exp(jax.random.uniform(streams[3], (ROWS, 1), jnp.float32, math.log(0.3), math.log(3.0)))
    key_scale = jnp.exp(jax.random.uniform(streams[4], (ROWS, 1), jnp.float32, math.log(0.3), math.log(3.0)))
    query_out = query_base * query_scale
    key_out = key_base * key_scale
    return (query_out, key_out)


def draw_query_rows(key, part):
    return draw_pair(key)[0].astype(jnp.bfloat16)


def draw_key_rows(key, part):
    return draw_pair(key)[1].astype(jnp.bfloat16)


def setup_inputs(seed: int = 0) -> dict:
    keys = jax.random.split(jax.random.key(seed), 4)
    query_rows = draw_query_rows(jax.random.fold_in(keys[3], 71), 0)
    key_rows = draw_key_rows(jax.random.fold_in(keys[3], 71), 0)
    partner = jax.vmap(lambda own: jax.random.permutation(own, BLK))(jax.random.split(keys[2], BLOCKS)).reshape((BLOCKS, BLK)).astype(jnp.int32)
    return {"query_rows": query_rows, "key_rows": key_rows, "partner": partner}


def fetch(table, index):
    return lax.dynamic_index_in_dim(table, index, 0, keepdims=False)


def log_total(values, axes):
    top = jnp.max(values, axis=axes, keepdims=True)
    summed = jnp.sum(jnp.exp(values - top), axis=axes, keepdims=True)
    return jnp.squeeze(top + jnp.log(summed), axis=axes)


def reference(query_rows, key_rows, partner):
    factor = float(D) ** -0.5
    query_blocks = query_rows.reshape(BLOCKS, BLK, D)
    key_blocks = key_rows.reshape(BLOCKS, BLK, D)
    indices = jnp.arange(BLOCKS, dtype=jnp.int32)
    columns = jnp.arange(BLK, dtype=jnp.int32)

    def window_scores(index):
        query_block = fetch(query_blocks, index)
        blocks = [fetch(key_blocks, (index - step) % BLOCKS) for step in range(WIN)]
        scores = jnp.stack([jnp.dot(query_block, block.T, preferred_element_type=jnp.float32) * factor for block in blocks])
        return scores, blocks

    def first_pass(index):
        scores, blocks = window_scores(index)
        return log_total(scores, (0, 2)), log_total(scores, (1,))

    row_lse, col_part = lax.map(first_pass, indices)
    shifted = jnp.stack([jnp.roll(col_part[:, step], -step, axis=0) for step in range(WIN)])
    col_lse = log_total(shifted, (0,))

    def partner_mask(index):
        chosen = fetch(partner, index)
        return (columns[None, :] == chosen[:, None]).astype(jnp.float32), chosen

    def second_pass(index):
        scores, blocks = window_scores(index)
        own_lse = fetch(row_lse, index)
        col_window = jnp.stack([fetch(col_lse, (index - step) % BLOCKS) for step in range(WIN)])
        mask, chosen = partner_mask(index)
        weights = 0.5 * jnp.exp(scores - own_lse[None, :, None]) + 0.5 * jnp.exp(scores - col_window[:, None, :])
        weights = weights - jnp.stack([mask] + [jnp.zeros_like(mask)] * (WIN - 1))
        weights = weights.astype(jnp.bfloat16)
        summed = jnp.zeros((BLK, D), jnp.float32)
        for step in range(WIN):
            summed = summed + jnp.dot(weights[step], blocks[step], preferred_element_type=jnp.float32)
        positive = jnp.take_along_axis(scores[0], chosen[:, None], axis=1)[:, 0]
        loss = 0.5 * own_lse + 0.5 * jnp.take(col_window[0], chosen) - positive
        return loss, summed * factor

    def third_pass(index):
        key_block = fetch(key_blocks, index)
        key_lse = fetch(col_lse, index)
        summed = jnp.zeros((BLK, D), jnp.float32)
        for step in range(WIN):
            source = (index + step) % BLOCKS
            query_block = fetch(query_blocks, source)
            scores = jnp.dot(query_block, key_block.T, preferred_element_type=jnp.float32) * factor
            weights = 0.5 * jnp.exp(scores - fetch(row_lse, source)[:, None]) + 0.5 * jnp.exp(scores - key_lse[None, :])
            if step == 0:
                weights = weights - partner_mask(index)[0]
            weights = weights.astype(jnp.bfloat16)
            summed = summed + jnp.dot(weights.T, query_block, preferred_element_type=jnp.float32)
        return summed * factor

    pair_loss, grad_queries = lax.map(second_pass, indices)
    grad_keys = lax.map(third_pass, indices)
    return pair_loss.reshape(ROWS), grad_queries.reshape(ROWS, D), grad_keys.reshape(ROWS, D)
```

```python
import functools

import jax
import jax.numpy as jnp
from jax import lax
from jax.experimental import pallas as pl
from jax.experimental.pallas import tpu as pltpu
from jax.sharding import PartitionSpec as P

F32 = jnp.float32
VMEM_LIMIT = 48 * 1024 * 1024
NT = (((1,), (1,)), ((), ()))


def shift(array, axis, move):
    peers = lax.axis_size(axis)
    return lax.ppermute(array, axis, [(i, move(i) % peers) for i in range(peers)])


def as_column(row):
    return jnp.broadcast_to(row, (128, row.shape[1])).T[:, 0:1]


def as_row(column):
    return jnp.broadcast_to(column, (column.shape[0], 128)).T[0:1, :]


def log_join(*parts):
    top = functools.reduce(jnp.maximum, parts)
    return top + jnp.log(sum(jnp.exp(part - top) for part in parts))


def fetch(sources, target, sems):
    rows = sources[0].shape[0]
    copies = []
    for i, source in enumerate(sources):
        copy = pltpu.make_async_copy(source, target.at[pl.ds(i * rows, rows)], sems.at[i])
        copy.start()
        copies.append(copy)
    return copies


def score_kernel(tokens, early, stats, factor, *refs):
    mine = refs[:2]
    shards = refs[2 : 2 + tokens]
    rest = list(refs[2 + tokens :])
    if stats:
        side = [rest.pop(0) for _ in range(2 if early else 1)]
    out = rest.pop(0)
    if stats:
        info = rest.pop(0)
    left, right, sems = rest
    copies = fetch(mine, left, sems) + fetch(shards, right, sems.at[pl.ds(2, tokens)])
    for copy in copies[:2]:
        copy.wait()
    rows = mine[0].shape[0]
    pair = 2 * rows
    lhs = left[...]
    row_parts = []
    for p in range(tokens // 2):
        copies[2 + 2 * p].wait()
        copies[3 + 2 * p].wait()
        s = lax.dot_general(
            lhs, right[pl.ds(p * pair, pair), :], NT, preferred_element_type=F32
        ) * factor
        out[:, pl.ds(p * pair, pair)] = s
        if stats:
            col_max = jnp.max(s, axis=0, keepdims=True)
            col = col_max + jnp.log(jnp.sum(jnp.exp(s - col_max), axis=0, keepdims=True))
            row_max = jnp.max(s, axis=1, keepdims=True)
            row_sum = jnp.sum(jnp.exp(s - row_max), axis=1, keepdims=True)
            row_parts.append(row_max + jnp.log(row_sum))
            info[pl.ds(p if early else 3, 1), :] = col
            if early and p == 0:
                hit = as_column(side[0][...]) == side[1][...]
                info[pl.ds(5, 1), :] = as_row(jnp.sum(jnp.where(hit, s, 0.0), axis=1, keepdims=True))
    if stats:
        row = as_row(log_join(*row_parts) if len(row_parts) > 1 else row_parts[0])
        if early:
            info[pl.ds(3, 1), :] = jnp.zeros((1, pair), F32)
            info[pl.ds(4, 1), :] = row
            info[pl.ds(6, 2), :] = jnp.zeros((2, pair), F32)
        else:
            info[pl.ds(0, 3), :] = side[0][pl.ds(0, 3), :]
            info[pl.ds(4, 1), :] = log_join(row, side[0][pl.ds(4, 1), :])
            info[pl.ds(5, 3), :] = side[0][pl.ds(5, 3), :]


def score(mine, shards, early, stats, factor, side=()):
    rows, width = mine[0].shape
    tokens = len(shards)
    anywhere = pl.BlockSpec(memory_space=pl.ANY)
    whole = pl.BlockSpec(memory_space=pltpu.VMEM)
    shapes = [jax.ShapeDtypeStruct((2 * rows, tokens * rows), F32)]
    if stats:
        shapes.append(jax.ShapeDtypeStruct((8, 2 * rows), F32))
    return pl.pallas_call(
        functools.partial(score_kernel, tokens, early, stats, factor),
        out_shape=tuple(shapes),
        in_specs=[anywhere] * (2 + tokens) + [whole] * len(side),
        out_specs=(whole,) * len(shapes),
        scratch_shapes=[
            pltpu.VMEM((2 * rows, width), jnp.bfloat16),
            pltpu.VMEM((tokens * rows, width), jnp.bfloat16),
            pltpu.SemaphoreType.DMA((2 + tokens,)),
        ],
        compiler_params=pltpu.CompilerParams(vmem_limit_bytes=VMEM_LIMIT),
        cost_estimate=pl.CostEstimate(
            flops=4 * rows * rows * tokens * width,
            bytes_accessed=(tokens + 2) * rows * width * 2 + 8 * rows * rows * tokens,
            transcendentals=4 * rows * rows * tokens if stats else 0,
        ),
    )(*mine, *shards, *side)


def halves(ref, row):
    n = ref.shape[1] // 2
    both = ref[pl.ds(row, 1), :]
    return both[:, :n], both[:, n:]


def by_shard(ref):
    a, b, early, late = (halves(ref, i) for i in range(4))
    return [a[0], a[1], b[0], b[1], early[0], late[0], early[1], late[1]]


def block_kernel(own, across, core, corner, out):
    for base, near, far in ((0, own, across), (8, core, corner)):
        near, far = by_shard(near), by_shard(far)
        for i in range(8):
            out[pl.ds(base + i, 1), :] = log_join(near[i], far[i ^ 1])
    own_row, core_row = halves(own, 4), halves(core, 4)
    across_row, corner_row = halves(across, 4), halves(corner, 4)
    out[pl.ds(16, 1), :] = log_join(own_row[0], core_row[1])
    out[pl.ds(17, 1), :] = log_join(across_row[0], corner_row[1])
    out[pl.ds(18, 1), :] = log_join(own_row[1], core_row[0])
    out[pl.ds(19, 1), :] = halves(own, 5)[0] + halves(core, 5)[1]
    out[pl.ds(20, 4), :] = jnp.zeros((4, out.shape[1]), F32)


def window_kernel(even_ref, ids, partner, *refs):
    around = dict(zip((0, 1, 2, 3, -1, -2, -3), refs[:7]))
    col_out, row_out, loss_out = refs[7:]
    even = even_ref[0] == 1

    def line(d, i):
        return around[d][pl.ds(i, 1), :]

    def pick(first, second):
        return jnp.where(even, first, second)

    def total(step, base, half):
        parts = []
        for other in range(4):
            d = other - step
            if other % 2 == 0:
                parts.append(line(d, base + other + half))
            else:
                c, e = line(d, base + 4 + half), line(d, base + 6 + half)
                c_first = (other == 1) == (d % 2 == 0)
                parts.append(pick(c, e) if c_first else pick(e, c))
        return log_join(*parts)

    sums = [[total(step, 0, half) for half in range(2)] for step in range(4)]
    core_sums = [total(0, 8, half) for half in range(2)]
    join = lambda first, second: jnp.concatenate([first, second], axis=1)
    c = [pick(sums[1][h], sums[3][h]) for h in range(2)]
    e = [pick(sums[3][h], sums[1][h]) for h in range(2)]
    col_out[pl.ds(0, 1), :] = join(*sums[0])
    col_out[pl.ds(1, 1), :] = join(*sums[2])
    col_out[pl.ds(2, 1), :] = join(c[0], e[0])
    col_out[pl.ds(3, 1), :] = join(c[1], e[1])
    col_out[pl.ds(4, 1), :] = join(sums[0][0], core_sums[0])
    near = [line(1, 16 + h) for h in range(2)]
    far = [line(3, 16 + h) for h in range(2)]
    c = [pick(far[h], near[h]) for h in range(2)]
    e = [pick(near[h], far[h]) for h in range(2)]
    row_out[pl.ds(0, 1), :] = join(line(0, 16), line(0, 17))
    row_out[pl.ds(1, 1), :] = join(line(2, 16), line(2, 17))
    row_out[pl.ds(2, 1), :] = join(c[0], e[0])
    row_out[pl.ds(3, 1), :] = join(c[1], e[1])
    row_out[pl.ds(4, 1), :] = join(line(0, 16), line(0, 18))
    zeros = jnp.zeros((3, col_out.shape[1]), F32)
    col_out[pl.ds(5, 3), :] = zeros
    row_out[pl.ds(5, 3), :] = zeros
    chosen = as_column(partner[...])
    found = jnp.zeros(chosen.shape, F32)
    for i, value in enumerate((sums[0][0], sums[0][1], core_sums[0], core_sums[1])):
        hit = chosen == ids[pl.ds(i, 1), :]
        found = found + jnp.sum(jnp.where(hit, value, 0.0), axis=1, keepdims=True)
    loss_out[...] = 0.5 * line(0, 16) + 0.5 * as_row(found) - line(0, 19)


def small_call(kernel, shapes, *args, scalars=0):
    whole = pl.BlockSpec(memory_space=pltpu.VMEM)
    return pl.pallas_call(
        kernel,
        out_shape=tuple(jax.ShapeDtypeStruct(s, F32) for s in shapes),
        in_specs=[pl.BlockSpec(memory_space=pltpu.SMEM)] * scalars + [whole] * (len(args) - scalars),
        out_specs=(whole,) * len(shapes),
        cost_estimate=pl.CostEstimate(flops=100000, bytes_accessed=400000, transcendentals=20000),
    )(*args)


def grad_kernel(group, factor, add, *refs):
    early, late, row_info, col_info, row_ids, col_ids = refs[:6]
    shards = refs[6:14]
    rest = list(refs[14:])
    received = rest.pop(0) if add else None
    out, s_early, s_late, held, weights, sems, s_sems = rest
    rows = out.shape[0]
    pair = 2 * rows
    here = pl.ds(group * rows, rows)
    s_copies = [
        pltpu.make_async_copy(early.at[here], s_early, s_sems.at[0]),
        pltpu.make_async_copy(late.at[here], s_late, s_sems.at[1]),
    ]
    for copy in s_copies:
        copy.start()
    copies = fetch(shards, held, sems)
    row = as_column(row_info[pl.ds(4, 1), :])[group * rows : (group + 1) * rows]
    own = as_column(row_ids[...])[group * rows : (group + 1) * rows]
    s_copies[0].wait()
    for p in range(4):
        if p < 3:
            s = s_early[:, pl.ds(p * pair, pair)]
        else:
            s_copies[1].wait()
            s = s_late[...]
        w = 0.5 * jnp.exp(s - row) + 0.5 * jnp.exp(s - col_info[pl.ds(p, 1), :])
        if p == 0:
            w = w - jnp.where(own == col_ids[...], 1.0, 0.0)
        weights[:, pl.ds(p * pair, pair)] = w.astype(jnp.bfloat16)
    for copy in copies:
        copy.wait()
    total = jnp.dot(weights[...], held[...], preferred_element_type=F32) * factor
    if add:
        total = total + received[...]
    out[...] = total


def grad(group, factor, early, late, row_info, col_info, row_ids, col_ids, shards, received=None):
    rows, width = shards[0].shape
    anywhere = pl.BlockSpec(memory_space=pl.ANY)
    whole = pl.BlockSpec(memory_space=pltpu.VMEM)
    add = received is not None
    return pl.pallas_call(
        functools.partial(grad_kernel, group, factor, add),
        out_shape=jax.ShapeDtypeStruct((rows, width), F32),
        in_specs=[anywhere] * 2 + [whole] * 4 + [anywhere] * 8 + ([whole] if add else []),
        out_specs=whole,
        scratch_shapes=[
            pltpu.VMEM((rows, 6 * rows), F32),
            pltpu.VMEM((rows, 2 * rows), F32),
            pltpu.VMEM((8 * rows, width), jnp.bfloat16),
            pltpu.VMEM((rows, 8 * rows), jnp.bfloat16),
            pltpu.SemaphoreType.DMA((8,)),
            pltpu.SemaphoreType.DMA((2,)),
        ],
        compiler_params=pltpu.CompilerParams(vmem_limit_bytes=VMEM_LIMIT),
        cost_estimate=pl.CostEstimate(
            flops=16 * rows * rows * width,
            bytes_accessed=8 * rows * width * 2 + 32 * rows * rows + rows * width * 4,
            transcendentals=16 * rows * rows,
        ),
    )(early, late, row_info, col_info, row_ids, col_ids, *shards, *((received,) if add else ()))


def local(query_rows, key_rows, partner):
    rows, features = query_rows.shape
    factor = float(features) ** (-0.5)
    block = lax.axis_index("blk")
    place = lax.axis_index("pb")
    even = block % 2 == 0

    across = lambda a: shift(a, "pb", lambda i: i ^ 2)
    core = lambda a: shift(a, "pb", lambda i: i ^ 1)
    corner = lambda a: shift(a, "pb", lambda i: i ^ 3)
    beside = lambda a: shift(a, "blk", lambda i: i ^ 1)
    ahead = lambda a: shift(a, "blk", lambda i: i + 2)
    back = lambda a: shift(a, "blk", lambda i: i - 2)
    apart = lambda a: shift(a, "blk", lambda i: i + 2 if i % 2 == 0 else i - 2)
    pick = lambda first, second: jnp.where(even, first, second)

    k0, q0 = key_rows, query_rows
    y1_in = pick(k0, q0)
    kx = across(k0)
    y1 = beside(y1_in)
    kz = ahead(k0)
    ks, qs = core(k0), core(q0)
    partner_core, partner_across = core(partner), across(partner)

    qx = across(q0)
    kzy = beside(kz)
    qz = back(q0)

    kzx = across(kz)
    qzy = beside(qz)
    m1 = apart(pick(kzy, qx))

    kd0 = pick(m1, y1)
    kd1 = across(kd0)
    kzxy = beside(kzx)
    m2 = back(pick(qx, qzy))

    qzx = pick(m2, m1)
    qd0 = pick(y1, m2)
    qd1 = across(qd0)
    qzxy = beside(qzx)

    lanes = jnp.arange(rows, dtype=jnp.int32)[None, :]
    id_own = place * rows + lanes
    id_across = (place ^ 2) * rows + lanes
    id_core = (place ^ 1) * rows + lanes
    id_corner = (place ^ 3) * rows + lanes
    q_row_ids = jnp.concatenate([partner, partner_core], axis=1)
    q_col_ids = jnp.concatenate([id_own, id_across], axis=1)
    k_row_ids = jnp.concatenate([id_own, id_core], axis=1)
    k_col_ids = jnp.concatenate([partner, partner_across], axis=1)
    ids = jnp.concatenate([id_own, id_across, id_core, id_corner], axis=0)

    k_shards = (k0, kx, kz, kzx, kzy, kd0, kzxy, kd1)
    q_shards = (q0, qx, qz, qzx, qzy, qd0, qzxy, qd1)
    s_early, info = score((q0, qs), k_shards[:6], True, True, factor, (q_row_ids, q_col_ids))
    s_late, info = score((q0, qs), k_shards[6:], False, True, factor, (info,))

    in_block = small_call(
        block_kernel, [(24, rows)], info, across(info), core(info), corner(info)
    )[0]
    near = [in_block] + [shift(in_block, "blk", lambda i, d=d: i - d) for d in (1, 2, 3, -1, -2, -3)]
    even_flag = even.astype(jnp.int32)[None]
    col_info, row_info, loss = small_call(
        window_kernel, [(8, 2 * rows), (8, 2 * rows), (1, rows)], even_flag, ids, partner, *near, scalars=1
    )
    (t_early,) = score((k0, ks), q_shards[:6], True, False, factor)
    (t_late,) = score((k0, ks), q_shards[6:], False, False, factor)

    q_args = (factor, s_early, s_late, row_info, col_info, q_row_ids, q_col_ids, k_shards)
    k_args = (factor, t_early, t_late, col_info, row_info, k_row_ids, k_col_ids, q_shards)
    q_other = core(grad(1, *q_args))
    k_other = core(grad(1, *k_args))
    grad_queries = grad(0, *q_args, q_other)
    grad_keys = grad(0, *k_args, k_other)
    return (loss[0], grad_queries, grad_keys)


def solution(mesh):
    return jax.shard_map(
        local,
        mesh=mesh,
        in_specs=(P(("blk", "pb"), None), P(("blk", "pb"), None), P("blk", "pb")),
        out_specs=(P(("blk", "pb")), P(("blk", "pb"), None), P(("blk", "pb"), None)),
        check_vma=False,
    )
```

```python
import functools

import jax
import jax.numpy as jnp
from jax import lax
from jax.experimental import pallas as pl
from jax.experimental.pallas import tpu as pltpu
from jax.sharding import PartitionSpec as P

F32 = jnp.float32
VMEM_LIMIT = 48 * 1024 * 1024
NT = (((1,), (1,)), ((), ()))


def shift(array, axis, move):
    peers = lax.axis_size(axis)
    return lax.ppermute(array, axis, [(i, move(i) % peers) for i in range(peers)])


def as_column(row):
    return jnp.broadcast_to(row, (128, row.shape[1])).T[:, 0:1]


def as_row(column):
    return jnp.broadcast_to(column, (column.shape[0], 128)).T[0:1, :]


def log_join(*parts):
    top = functools.reduce(jnp.maximum, parts)
    return top + jnp.log(sum(jnp.exp(part - top) for part in parts))


def fetch(sources, target, sems):
    rows = sources[0].shape[0]
    copies = []
    for i, source in enumerate(sources):
        copy = pltpu.make_async_copy(source, target.at[pl.ds(i * rows, rows)], sems.at[i])
        copy.start()
        copies.append(copy)
    return copies


def choose_kernel(flag, first, second, out, sem):
    @pl.when(flag[0] == 1)
    def _():
        pltpu.make_async_copy(first, out, sem).start()

    @pl.when(flag[0] != 1)
    def _():
        pltpu.make_async_copy(second, out, sem).start()

    pltpu.make_async_copy(first, out, sem).wait()


def choose(flag, first, second):
    anywhere = pl.BlockSpec(memory_space=pl.ANY)
    return pl.pallas_call(
        choose_kernel,
        out_shape=jax.ShapeDtypeStruct(first.shape, first.dtype),
        in_specs=[pl.BlockSpec(memory_space=pltpu.SMEM), anywhere, anywhere],
        out_specs=anywhere,
        scratch_shapes=[pltpu.SemaphoreType.DMA],
        cost_estimate=pl.CostEstimate(flops=0, bytes_accessed=2 * first.size * 2, transcendentals=0),
    )(flag, first, second)


def after(values, landed):
    done = lax.optimization_barrier((values, landed))
    return done[0], done[1]


def score_kernel(tokens, early, stats, factor, *refs):
    mine = refs[:2]
    shards = refs[2 : 2 + tokens]
    rest = list(refs[2 + tokens :])
    if stats:
        side = [rest.pop(0) for _ in range(2 if early else 1)]
    out = rest.pop(0)
    if stats:
        info = rest.pop(0)
    left, right, sems = rest
    copies = fetch(mine, left, sems) + fetch(shards, right, sems.at[pl.ds(2, tokens)])
    for copy in copies[:2]:
        copy.wait()
    rows = mine[0].shape[0]
    pair = 2 * rows
    lhs = left[...]
    row_parts = []
    for p in range(tokens // 2):
        copies[2 + 2 * p].wait()
        copies[3 + 2 * p].wait()
        s = lax.dot_general(
            lhs, right[pl.ds(p * pair, pair), :], NT, preferred_element_type=F32
        ) * factor
        out[:, pl.ds(p * pair, pair)] = s
        if stats:
            col_max = jnp.max(s, axis=0, keepdims=True)
            col = col_max + jnp.log(jnp.sum(jnp.exp(s - col_max), axis=0, keepdims=True))
            row_max = jnp.max(s, axis=1, keepdims=True)
            row_sum = jnp.sum(jnp.exp(s - row_max), axis=1, keepdims=True)
            row_parts.append(row_max + jnp.log(row_sum))
            info[pl.ds(p if early else 3, 1), :] = col
            if early and p == 0:
                hit = as_column(side[0][...]) == side[1][...]
                info[pl.ds(5, 1), :] = as_row(jnp.sum(jnp.where(hit, s, 0.0), axis=1, keepdims=True))
    if stats:
        row = as_row(log_join(*row_parts) if len(row_parts) > 1 else row_parts[0])
        if early:
            info[pl.ds(3, 1), :] = jnp.zeros((1, pair), F32)
            info[pl.ds(4, 1), :] = row
            info[pl.ds(6, 2), :] = jnp.zeros((2, pair), F32)
        else:
            info[pl.ds(0, 3), :] = side[0][pl.ds(0, 3), :]
            info[pl.ds(4, 1), :] = log_join(row, side[0][pl.ds(4, 1), :])
            info[pl.ds(5, 3), :] = side[0][pl.ds(5, 3), :]


def score(mine, shards, early, stats, factor, side=()):
    rows, width = mine[0].shape
    tokens = len(shards)
    anywhere = pl.BlockSpec(memory_space=pl.ANY)
    whole = pl.BlockSpec(memory_space=pltpu.VMEM)
    shapes = [jax.ShapeDtypeStruct((2 * rows, tokens * rows), F32)]
    if stats:
        shapes.append(jax.ShapeDtypeStruct((8, 2 * rows), F32))
    return pl.pallas_call(
        functools.partial(score_kernel, tokens, early, stats, factor),
        out_shape=tuple(shapes),
        in_specs=[anywhere] * (2 + tokens) + [whole] * len(side),
        out_specs=(whole,) * len(shapes),
        scratch_shapes=[
            pltpu.VMEM((2 * rows, width), jnp.bfloat16),
            pltpu.VMEM((tokens * rows, width), jnp.bfloat16),
            pltpu.SemaphoreType.DMA((2 + tokens,)),
        ],
        compiler_params=pltpu.CompilerParams(vmem_limit_bytes=VMEM_LIMIT),
        cost_estimate=pl.CostEstimate(
            flops=4 * rows * rows * tokens * width,
            bytes_accessed=(tokens + 2) * rows * width * 2 + 8 * rows * rows * tokens,
            transcendentals=4 * rows * rows * tokens if stats else 0,
        ),
    )(*mine, *shards, *side)


def halves(ref, row):
    n = ref.shape[1] // 2
    both = ref[pl.ds(row, 1), :]
    return both[:, :n], both[:, n:]


def by_shard(ref):
    a, b, early, late = (halves(ref, i) for i in range(4))
    return [a[0], a[1], b[0], b[1], early[0], late[0], early[1], late[1]]


def block_kernel(own, across, core, corner, out):
    for base, near, far in ((0, own, across), (8, core, corner)):
        near, far = by_shard(near), by_shard(far)
        for i in range(8):
            out[pl.ds(base + i, 1), :] = log_join(near[i], far[i ^ 1])
    own_row, core_row = halves(own, 4), halves(core, 4)
    across_row, corner_row = halves(across, 4), halves(corner, 4)
    out[pl.ds(16, 1), :] = log_join(own_row[0], core_row[1])
    out[pl.ds(17, 1), :] = log_join(across_row[0], corner_row[1])
    out[pl.ds(18, 1), :] = log_join(own_row[1], core_row[0])
    out[pl.ds(19, 1), :] = halves(own, 5)[0] + halves(core, 5)[1]
    out[pl.ds(20, 4), :] = jnp.zeros((4, out.shape[1]), F32)


def window_kernel(even_ref, ids, partner, *refs):
    around = dict(zip((0, 1, 2, 3, -1, -2, -3), refs[:7]))
    col_out, row_out, loss_out = refs[7:]
    even = even_ref[0] == 1

    def line(d, i):
        return around[d][pl.ds(i, 1), :]

    def pick(first, second):
        return jnp.where(even, first, second)

    def total(step, base, half):
        parts = []
        for other in range(4):
            d = other - step
            if other % 2 == 0:
                parts.append(line(d, base + other + half))
            else:
                c, e = line(d, base + 4 + half), line(d, base + 6 + half)
                c_first = (other == 1) == (d % 2 == 0)
                parts.append(pick(c, e) if c_first else pick(e, c))
        return log_join(*parts)

    sums = [[total(step, 0, half) for half in range(2)] for step in range(4)]
    core_sums = [total(0, 8, half) for half in range(2)]
    join = lambda first, second: jnp.concatenate([first, second], axis=1)
    c = [pick(sums[1][h], sums[3][h]) for h in range(2)]
    e = [pick(sums[3][h], sums[1][h]) for h in range(2)]
    col_out[pl.ds(0, 1), :] = join(*sums[0])
    col_out[pl.ds(1, 1), :] = join(*sums[2])
    col_out[pl.ds(2, 1), :] = join(c[0], e[0])
    col_out[pl.ds(3, 1), :] = join(c[1], e[1])
    col_out[pl.ds(4, 1), :] = join(sums[0][0], core_sums[0])
    near = [line(1, 16 + h) for h in range(2)]
    far = [line(3, 16 + h) for h in range(2)]
    c = [pick(far[h], near[h]) for h in range(2)]
    e = [pick(near[h], far[h]) for h in range(2)]
    row_out[pl.ds(0, 1), :] = join(line(0, 16), line(0, 17))
    row_out[pl.ds(1, 1), :] = join(line(2, 16), line(2, 17))
    row_out[pl.ds(2, 1), :] = join(c[0], e[0])
    row_out[pl.ds(3, 1), :] = join(c[1], e[1])
    row_out[pl.ds(4, 1), :] = join(line(0, 16), line(0, 18))
    zeros = jnp.zeros((3, col_out.shape[1]), F32)
    col_out[pl.ds(5, 3), :] = zeros
    row_out[pl.ds(5, 3), :] = zeros
    chosen = as_column(partner[...])
    found = jnp.zeros(chosen.shape, F32)
    for i, value in enumerate((sums[0][0], sums[0][1], core_sums[0], core_sums[1])):
        hit = chosen == ids[pl.ds(i, 1), :]
        found = found + jnp.sum(jnp.where(hit, value, 0.0), axis=1, keepdims=True)
    loss_out[...] = 0.5 * line(0, 16) + 0.5 * as_row(found) - line(0, 19)


def small_call(kernel, shapes, *args, scalars=0):
    whole = pl.BlockSpec(memory_space=pltpu.VMEM)
    return pl.pallas_call(
        kernel,
        out_shape=tuple(jax.ShapeDtypeStruct(s, F32) for s in shapes),
        in_specs=[pl.BlockSpec(memory_space=pltpu.SMEM)] * scalars + [whole] * (len(args) - scalars),
        out_specs=(whole,) * len(shapes),
        cost_estimate=pl.CostEstimate(flops=100000, bytes_accessed=400000, transcendentals=20000),
    )(*args)


def grad_kernel(group, factor, add, *refs):
    early, late, row_info, col_info, row_ids, col_ids = refs[:6]
    shards = refs[6:14]
    rest = list(refs[14:])
    received = rest.pop(0) if add else None
    out, s_early, s_late, held, weights, sems, s_sems = rest
    rows = out.shape[0]
    pair = 2 * rows
    here = pl.ds(group * rows, rows)
    s_copies = [
        pltpu.make_async_copy(early.at[here], s_early, s_sems.at[0]),
        pltpu.make_async_copy(late.at[here], s_late, s_sems.at[1]),
    ]
    for copy in s_copies:
        copy.start()
    copies = fetch(shards, held, sems)
    row = as_column(row_info[pl.ds(4, 1), :])[group * rows : (group + 1) * rows]
    own = as_column(row_ids[...])[group * rows : (group + 1) * rows]
    s_copies[0].wait()
    for p in range(4):
        if p < 3:
            s = s_early[:, pl.ds(p * pair, pair)]
        else:
            s_copies[1].wait()
            s = s_late[...]
        w = 0.5 * jnp.exp(s - row) + 0.5 * jnp.exp(s - col_info[pl.ds(p, 1), :])
        if p == 0:
            w = w - jnp.where(own == col_ids[...], 1.0, 0.0)
        weights[:, pl.ds(p * pair, pair)] = w.astype(jnp.bfloat16)
    for copy in copies:
        copy.wait()
    total = jnp.dot(weights[...], held[...], preferred_element_type=F32) * factor
    if add:
        total = total + received[...]
    out[...] = total


def grad(group, factor, early, late, row_info, col_info, row_ids, col_ids, shards, received=None):
    rows, width = shards[0].shape
    anywhere = pl.BlockSpec(memory_space=pl.ANY)
    whole = pl.BlockSpec(memory_space=pltpu.VMEM)
    add = received is not None
    return pl.pallas_call(
        functools.partial(grad_kernel, group, factor, add),
        out_shape=jax.ShapeDtypeStruct((rows, width), F32),
        in_specs=[anywhere] * 2 + [whole] * 4 + [anywhere] * 8 + ([whole] if add else []),
        out_specs=whole,
        scratch_shapes=[
            pltpu.VMEM((rows, 6 * rows), F32),
            pltpu.VMEM((rows, 2 * rows), F32),
            pltpu.VMEM((8 * rows, width), jnp.bfloat16),
            pltpu.VMEM((rows, 8 * rows), jnp.bfloat16),
            pltpu.SemaphoreType.DMA((8,)),
            pltpu.SemaphoreType.DMA((2,)),
        ],
        compiler_params=pltpu.CompilerParams(vmem_limit_bytes=VMEM_LIMIT),
        cost_estimate=pl.CostEstimate(
            flops=16 * rows * rows * width,
            bytes_accessed=8 * rows * width * 2 + 32 * rows * rows + rows * width * 4,
            transcendentals=16 * rows * rows,
        ),
    )(early, late, row_info, col_info, row_ids, col_ids, *shards, *((received,) if add else ()))


def local(query_rows, key_rows, partner):
    rows, features = query_rows.shape
    factor = float(features) ** (-0.5)
    block = lax.axis_index("blk")
    place = lax.axis_index("pb")
    even = block % 2 == 0

    across = lambda a: shift(a, "pb", lambda i: i ^ 2)
    core = lambda a: shift(a, "pb", lambda i: i ^ 1)
    corner = lambda a: shift(a, "pb", lambda i: i ^ 3)
    beside = lambda a: shift(a, "blk", lambda i: i ^ 1)
    ahead = lambda a: shift(a, "blk", lambda i: i + 2)
    back = lambda a: shift(a, "blk", lambda i: i - 2)
    apart = lambda a: shift(a, "blk", lambda i: i + 2 if i % 2 == 0 else i - 2)
    flag = even.astype(jnp.int32)[None]
    pick = functools.partial(choose, flag)

    k0, q0 = key_rows, query_rows
    kx, kz, y1 = across(k0), ahead(k0), beside(pick(k0, q0))
    ks, qs = core(k0), core(q0)
    partner_core, partner_across = core(partner), across(partner)
    (q0b, kzb), (kx, kz, y1) = after((q0, kz), (kx, kz, y1))
    qx, kzy, qz = across(q0b), beside(kzb), back(q0b)
    (kzb, qzb, kzyb, qxb), (qx, kzy, qz) = after((kz, qz, kzy, qx), (qx, kzy, qz))
    kzx, qzy, m1 = across(kzb), beside(qzb), apart(pick(kzyb, qxb))
    (m1b, y1b, kzxb, qxb, qzyb), (kzx, qzy, m1) = after((m1, y1, kzx, qx, qzy), (kzx, qzy, m1))
    kd0 = pick(m1b, y1b)
    kd1, kzxy, m2 = across(kd0), beside(kzxb), back(pick(qxb, qzyb))
    (y1b, m1b, m2b), (kd1, kzxy, m2) = after((y1, m1, m2), (kd1, kzxy, m2))
    qd0, qzx = pick(y1b, m2b), pick(m2b, m1b)
    qd1, qzxy = across(qd0), beside(qzx)

    lanes = jnp.arange(rows, dtype=jnp.int32)[None, :]
    id_own = place * rows + lanes
    id_across = (place ^ 2) * rows + lanes
    id_core = (place ^ 1) * rows + lanes
    id_corner = (place ^ 3) * rows + lanes
    q_row_ids = jnp.concatenate([partner, partner_core], axis=1)
    q_col_ids = jnp.concatenate([id_own, id_across], axis=1)
    k_row_ids = jnp.concatenate([id_own, id_core], axis=1)
    k_col_ids = jnp.concatenate([partner, partner_across], axis=1)
    ids = jnp.concatenate([id_own, id_across, id_core, id_corner], axis=0)

    k_shards = (k0, kx, kz, kzx, kzy, kd0, kzxy, kd1)
    q_shards = (q0, qx, qz, qzx, qzy, qd0, qzxy, qd1)
    s_early, info = score((q0, qs), k_shards[:6], True, True, factor, (q_row_ids, q_col_ids))
    s_late, info = score((q0, qs), k_shards[6:], False, True, factor, (info,))

    in_block = small_call(
        block_kernel, [(24, rows)], info, across(info), core(info), corner(info)
    )[0]
    near = [in_block] + [shift(in_block, "blk", lambda i, d=d: i - d) for d in (1, 2, 3, -1, -2, -3)]
    col_info, row_info, loss = small_call(
        window_kernel, [(8, 2 * rows), (8, 2 * rows), (1, rows)], flag, ids, partner, *near, scalars=1
    )
    (t_early,) = score((k0, ks), q_shards[:6], True, False, factor)
    (t_late,) = score((k0, ks), q_shards[6:], False, False, factor)

    q_args = (factor, s_early, s_late, row_info, col_info, q_row_ids, q_col_ids, k_shards)
    k_args = (factor, t_early, t_late, col_info, row_info, k_row_ids, k_col_ids, q_shards)
    q_other = core(grad(1, *q_args))
    k_other = core(grad(1, *k_args))
    grad_queries = grad(0, *q_args, q_other)
    grad_keys = grad(0, *k_args, k_other)
    return (loss[0], grad_queries, grad_keys)


def solution(mesh):
    return jax.shard_map(
        local,
        mesh=mesh,
        in_specs=(P(("blk", "pb"), None), P(("blk", "pb"), None), P("blk", "pb")),
        out_specs=(P(("blk", "pb")), P(("blk", "pb"), None), P(("blk", "pb"), None)),
        check_vma=False,
    )
```

```python
import functools

import jax
import jax.numpy as jnp
from jax import lax
from jax.experimental import pallas as pl
from jax.experimental.pallas import tpu as pltpu
from jax.sharding import PartitionSpec as P

F32 = jnp.float32
VMEM_LIMIT = 20 * 1024 * 1024
ANYWHERE = pl.BlockSpec(memory_space=pl.ANY)
WHOLE = pl.BlockSpec(memory_space=pltpu.VMEM)
NT = (((1,), (1,)), ((), ()))


def shift(array, axis, move):
    peers = lax.axis_size(axis)
    return lax.ppermute(array, axis, [(i, move(i) % peers) for i in range(peers)])


def as_column(row):
    return jnp.broadcast_to(row, (128, row.shape[1])).T[:, 0:1]


def as_row(column):
    return jnp.broadcast_to(column, (column.shape[0], 128)).T[0:1, :]


def log_join(*parts):
    top = functools.reduce(jnp.maximum, parts)
    return top + jnp.log(sum(jnp.exp(part - top) for part in parts))


def fetch(sources, target, sems):
    rows = sources[0].shape[0]
    copies = []
    for i, source in enumerate(sources):
        copy = pltpu.make_async_copy(source, target.at[pl.ds(i * rows, rows)], sems.at[i])
        copy.start()
        copies.append(copy)
    return copies


def choose_kernel(flag, first, second, out, sem):
    @pl.when(flag[0] == 1)
    def _():
        pltpu.make_async_copy(first, out, sem).start()

    @pl.when(flag[0] != 1)
    def _():
        pltpu.make_async_copy(second, out, sem).start()

    pltpu.make_async_copy(first, out, sem).wait()


def choose(flag, first, second):
    return pl.pallas_call(
        choose_kernel,
        out_shape=jax.ShapeDtypeStruct(first.shape, first.dtype),
        in_specs=[pl.BlockSpec(memory_space=pltpu.SMEM), ANYWHERE, ANYWHERE],
        out_specs=WHOLE,
        scratch_shapes=[pltpu.SemaphoreType.DMA],
        compiler_params=pltpu.CompilerParams(vmem_limit_bytes=VMEM_LIMIT),
        cost_estimate=pl.CostEstimate(flops=0, bytes_accessed=2 * first.size * 2, transcendentals=0),
    )(flag, first, second)


def after(value, landed):
    return lax.optimization_barrier((value, landed))[0]


def kept(shape, dtype):
    return pltpu.VMEM(shape, dtype)


def in_vmem(array):
    return pltpu.with_memory_space_constraint(array, pltpu.VMEM)


def score_kernel(tokens, early, stats, factor, *refs):
    mine = refs[:2]
    shards = refs[2 : 2 + tokens]
    rest = list(refs[2 + tokens :])
    if stats:
        side = [rest.pop(0) for _ in range(2 if early else 1)]
    out, right = rest.pop(0), rest.pop(0)
    if stats:
        info = rest.pop(0)
    left, sems = rest
    copies = fetch(mine, left, sems) + fetch(shards, right, sems.at[pl.ds(2, tokens)])
    for copy in copies[:2]:
        copy.wait()
    rows = mine[0].shape[0]
    pair = 2 * rows
    lhs = left[...]
    row_parts = []
    for p in range(tokens // 2):
        copies[2 + 2 * p].wait()
        copies[3 + 2 * p].wait()
        s = lax.dot_general(
            lhs, right[pl.ds(p * pair, pair), :], NT, preferred_element_type=F32
        ) * factor
        out[:, pl.ds(p * pair, pair)] = s
        if stats:
            col_max = jnp.max(s, axis=0, keepdims=True)
            col = col_max + jnp.log(jnp.sum(jnp.exp(s - col_max), axis=0, keepdims=True))
            row_max = jnp.max(s, axis=1, keepdims=True)
            row_sum = jnp.sum(jnp.exp(s - row_max), axis=1, keepdims=True)
            row_parts.append(row_max + jnp.log(row_sum))
            info[pl.ds(p if early else 3, 1), :] = col
            if early and p == 0:
                hit = as_column(side[0][...]) == side[1][...]
                info[pl.ds(5, 1), :] = as_row(jnp.sum(jnp.where(hit, s, 0.0), axis=1, keepdims=True))
    if stats:
        row = as_row(log_join(*row_parts) if len(row_parts) > 1 else row_parts[0])
        if early:
            info[pl.ds(3, 1), :] = jnp.zeros((1, pair), F32)
            info[pl.ds(4, 1), :] = row
            info[pl.ds(6, 2), :] = jnp.zeros((2, pair), F32)
        else:
            info[pl.ds(0, 3), :] = side[0][pl.ds(0, 3), :]
            info[pl.ds(4, 1), :] = log_join(row, side[0][pl.ds(4, 1), :])
            info[pl.ds(5, 3), :] = side[0][pl.ds(5, 3), :]


def score(mine, shards, early, stats, factor, side=()):
    rows, width = mine[0].shape
    tokens = len(shards)
    shapes = [kept((2 * rows, tokens * rows), F32), kept((tokens * rows, width), jnp.bfloat16)]
    if stats:
        shapes.append(jax.ShapeDtypeStruct((8, 2 * rows), F32))
    return pl.pallas_call(
        functools.partial(score_kernel, tokens, early, stats, factor),
        out_shape=tuple(shapes),
        in_specs=[ANYWHERE] * (2 + tokens) + [WHOLE] * len(side),
        out_specs=(WHOLE,) * len(shapes),
        scratch_shapes=[
            pltpu.VMEM((2 * rows, width), jnp.bfloat16),
            pltpu.SemaphoreType.DMA((2 + tokens,)),
        ],
        compiler_params=pltpu.CompilerParams(vmem_limit_bytes=VMEM_LIMIT),
        cost_estimate=pl.CostEstimate(
            flops=4 * rows * rows * tokens * width,
            bytes_accessed=(tokens + 2) * rows * width * 2 + 8 * rows * rows * tokens,
            transcendentals=4 * rows * rows * tokens if stats else 0,
        ),
    )(*mine, *shards, *side)


def halves(ref, row):
    n = ref.shape[1] // 2
    both = ref[pl.ds(row, 1), :]
    return both[:, :n], both[:, n:]


def by_shard(ref):
    a, b, early, late = (halves(ref, i) for i in range(4))
    return [a[0], a[1], b[0], b[1], early[0], late[0], early[1], late[1]]


def block_kernel(own, across, core, corner, out):
    for base, near, far in ((0, own, across), (8, core, corner)):
        near, far = by_shard(near), by_shard(far)
        for i in range(8):
            out[pl.ds(base + i, 1), :] = log_join(near[i], far[i ^ 1])
    own_row, core_row = halves(own, 4), halves(core, 4)
    across_row, corner_row = halves(across, 4), halves(corner, 4)
    out[pl.ds(16, 1), :] = log_join(own_row[0], core_row[1])
    out[pl.ds(17, 1), :] = log_join(across_row[0], corner_row[1])
    out[pl.ds(18, 1), :] = log_join(own_row[1], core_row[0])
    out[pl.ds(19, 1), :] = halves(own, 5)[0] + halves(core, 5)[1]
    out[pl.ds(20, 4), :] = jnp.zeros((4, out.shape[1]), F32)


def window_kernel(even_ref, ids, partner, *refs):
    around = dict(zip((0, 1, 2, 3, -1, -2, -3), refs[:7]))
    col_out, row_out, loss_out = refs[7:]
    even = even_ref[0] == 1

    def line(d, i):
        return around[d][pl.ds(i, 1), :]

    def pick(first, second):
        return jnp.where(even, first, second)

    def total(step, base, half):
        parts = []
        for other in range(4):
            d = other - step
            if other % 2 == 0:
                parts.append(line(d, base + other + half))
            else:
                c, e = line(d, base + 4 + half), line(d, base + 6 + half)
                c_first = (other == 1) == (d % 2 == 0)
                parts.append(pick(c, e) if c_first else pick(e, c))
        return log_join(*parts)

    sums = [[total(step, 0, half) for half in range(2)] for step in range(4)]
    core_sums = [total(0, 8, half) for half in range(2)]
    join = lambda first, second: jnp.concatenate([first, second], axis=1)
    c = [pick(sums[1][h], sums[3][h]) for h in range(2)]
    e = [pick(sums[3][h], sums[1][h]) for h in range(2)]
    col_out[pl.ds(0, 1), :] = join(*sums[0])
    col_out[pl.ds(1, 1), :] = join(*sums[2])
    col_out[pl.ds(2, 1), :] = join(c[0], e[0])
    col_out[pl.ds(3, 1), :] = join(c[1], e[1])
    col_out[pl.ds(4, 1), :] = join(sums[0][0], core_sums[0])
    near = [line(1, 16 + h) for h in range(2)]
    far = [line(3, 16 + h) for h in range(2)]
    c = [pick(far[h], near[h]) for h in range(2)]
    e = [pick(near[h], far[h]) for h in range(2)]
    row_out[pl.ds(0, 1), :] = join(line(0, 16), line(0, 17))
    row_out[pl.ds(1, 1), :] = join(line(2, 16), line(2, 17))
    row_out[pl.ds(2, 1), :] = join(c[0], e[0])
    row_out[pl.ds(3, 1), :] = join(c[1], e[1])
    row_out[pl.ds(4, 1), :] = join(line(0, 16), line(0, 18))
    zeros = jnp.zeros((3, col_out.shape[1]), F32)
    col_out[pl.ds(5, 3), :] = zeros
    row_out[pl.ds(5, 3), :] = zeros
    chosen = as_column(partner[...])
    found = jnp.zeros(chosen.shape, F32)
    for i, value in enumerate((sums[0][0], sums[0][1], core_sums[0], core_sums[1])):
        hit = chosen == ids[pl.ds(i, 1), :]
        found = found + jnp.sum(jnp.where(hit, value, 0.0), axis=1, keepdims=True)
    loss_out[...] = 0.5 * line(0, 16) + 0.5 * as_row(found) - line(0, 19)


def small_call(kernel, shapes, *args, scalars=0):
    return pl.pallas_call(
        kernel,
        out_shape=tuple(jax.ShapeDtypeStruct(s, F32) for s in shapes),
        in_specs=[pl.BlockSpec(memory_space=pltpu.SMEM)] * scalars + [WHOLE] * (len(args) - scalars),
        out_specs=(WHOLE,) * len(shapes),
        compiler_params=pltpu.CompilerParams(vmem_limit_bytes=VMEM_LIMIT),
        cost_estimate=pl.CostEstimate(flops=100000, bytes_accessed=400000, transcendentals=20000),
    )(*args)


def grad_kernel(group, factor, add, *refs):
    early, late, held_early, held_late, row_info, col_info, row_ids, col_ids = refs[:8]
    received = refs[8] if add else None
    out, weights = refs[-2:]
    rows = out.shape[0]
    pair = 2 * rows
    here = pl.ds(group * rows, rows)
    row = as_column(row_info[pl.ds(4, 1), :])[group * rows : (group + 1) * rows]
    own = as_column(row_ids[...])[group * rows : (group + 1) * rows]
    for p in range(4):
        s = early[here, pl.ds(p * pair, pair)] if p < 3 else late[here, :]
        w = 0.5 * jnp.exp(s - row) + 0.5 * jnp.exp(s - col_info[pl.ds(p, 1), :])
        if p == 0:
            w = w - jnp.where(own == col_ids[...], 1.0, 0.0)
        weights[:, pl.ds(p * pair, pair)] = w.astype(jnp.bfloat16)
    total = jnp.dot(weights[:, pl.ds(0, 3 * pair)], held_early[...], preferred_element_type=F32)
    total = total + jnp.dot(weights[:, pl.ds(3 * pair, pair)], held_late[...], preferred_element_type=F32)
    total = total * factor
    if add:
        total = total + received[...]
    out[...] = total


def grad(group, factor, parts, row_info, col_info, row_ids, col_ids, received=None):
    rows, width = parts[0].shape[0] // 2, parts[2].shape[1]
    add = received is not None
    return pl.pallas_call(
        functools.partial(grad_kernel, group, factor, add),
        out_shape=jax.ShapeDtypeStruct((rows, width), F32),
        in_specs=[WHOLE] * (9 if add else 8),
        out_specs=WHOLE,
        scratch_shapes=[pltpu.VMEM((rows, 8 * rows), jnp.bfloat16)],
        compiler_params=pltpu.CompilerParams(vmem_limit_bytes=VMEM_LIMIT),
        cost_estimate=pl.CostEstimate(
            flops=16 * rows * rows * width,
            bytes_accessed=8 * rows * width * 2 + 32 * rows * rows + rows * width * 4,
            transcendentals=16 * rows * rows,
        ),
    )(*map(in_vmem, parts), row_info, col_info, row_ids, col_ids, *((received,) if add else ()))


def local(query_rows, key_rows, partner):
    rows, features = query_rows.shape
    factor = float(features) ** (-0.5)
    block = lax.axis_index("blk")
    place = lax.axis_index("pb")
    even = block % 2 == 0

    across = lambda a: shift(a, "pb", lambda i: i ^ 2)
    core = lambda a: shift(a, "pb", lambda i: i ^ 1)
    corner = lambda a: shift(a, "pb", lambda i: i ^ 3)
    beside = lambda a: shift(a, "blk", lambda i: i ^ 1)
    ahead = lambda a: shift(a, "blk", lambda i: i + 2)
    back = lambda a: shift(a, "blk", lambda i: i - 2)
    apart = lambda a: shift(a, "blk", lambda i: i + 2 if i % 2 == 0 else i - 2)
    flag = even.astype(jnp.int32)[None]
    pick = functools.partial(choose, flag)

    k0, q0 = key_rows, query_rows
    kx, kz, y1 = across(k0), ahead(k0), beside(pick(k0, q0))
    ks, qs = core(k0), core(q0)
    partner_core, partner_across = core(partner), across(partner)

    qx = across(after(q0, kx))
    kzy = beside(after(kz, y1))
    qz = back(after(q0, kz))

    kzx = across(after(kz, qx))
    qzy = beside(after(qz, kzy))
    m1 = apart(after(pick(kzy, qx), qz))

    kd0 = pick(m1, y1)
    kd1 = across(after(kd0, kzx))
    kzxy = beside(after(kzx, qzy))
    m2 = back(after(pick(qx, qzy), m1))

    qd0, qzx = pick(y1, m2), pick(m2, m1)
    qd1 = across(after(qd0, kd1))
    qzxy = beside(after(qzx, kzxy))

    lanes = jnp.arange(rows, dtype=jnp.int32)[None, :]
    id_own = place * rows + lanes
    id_across = (place ^ 2) * rows + lanes
    id_core = (place ^ 1) * rows + lanes
    id_corner = (place ^ 3) * rows + lanes
    q_row_ids = jnp.concatenate([partner, partner_core], axis=1)
    q_col_ids = jnp.concatenate([id_own, id_across], axis=1)
    k_row_ids = jnp.concatenate([id_own, id_core], axis=1)
    k_col_ids = jnp.concatenate([partner, partner_across], axis=1)
    ids = jnp.concatenate([id_own, id_across, id_core, id_corner], axis=0)

    k_shards = (k0, kx, kz, kzx, kzy, kd0, kzxy, kd1)
    q_shards = (q0, qx, qz, qzx, qzy, qd0, qzxy, qd1)
    s_early, k_early, info = score((q0, qs), k_shards[:6], True, True, factor, (q_row_ids, q_col_ids))
    s_late, k_late, info = score((q0, qs), k_shards[6:], False, True, factor, (info,))

    in_block = small_call(
        block_kernel, [(24, rows)], info, across(info), core(info), corner(info)
    )[0]
    near = [in_block] + [shift(in_block, "blk", lambda i, d=d: i - d) for d in (1, 2, 3, -1, -2, -3)]
    col_info, row_info, loss = small_call(
        window_kernel, [(8, 2 * rows), (8, 2 * rows), (1, rows)], flag, ids, partner, *near, scalars=1
    )
    t_early, q_early = score((k0, ks), q_shards[:6], True, False, factor)
    t_late, q_late = score((k0, ks), q_shards[6:], False, False, factor)

    q_args = (factor, (s_early, s_late, k_early, k_late), row_info, col_info, q_row_ids, q_col_ids)
    k_args = (factor, (t_early, t_late, q_early, q_late), col_info, row_info, k_row_ids, k_col_ids)
    q_other = core(grad(1, *q_args))
    k_other = core(grad(1, *k_args))
    grad_queries = grad(0, *q_args, q_other)
    grad_keys = grad(0, *k_args, k_other)
    return (loss[0], grad_queries, grad_keys)


def solution(mesh):
    return jax.shard_map(
        local,
        mesh=mesh,
        in_specs=(P(("blk", "pb"), None), P(("blk", "pb"), None), P("blk", "pb")),
        out_specs=(P(("blk", "pb")), P(("blk", "pb"), None), P(("blk", "pb"), None)),
        check_vma=False,
    )
```

```python
import functools

import jax
import jax.numpy as jnp
from jax import lax
from jax.experimental import pallas as pl
from jax.experimental.pallas import tpu as pltpu
from jax.sharding import PartitionSpec as P

F32 = jnp.float32
BLOCK_AXIS, PART_AXIS = "blk", "pb"
CUTS = (96, 192)
VMEM_LIMIT = 16 * 1024 * 1024
ANYWHERE = pl.BlockSpec(memory_space=pl.ANY)
WHOLE = pl.BlockSpec(memory_space=pltpu.VMEM)
SCALAR = pl.BlockSpec(memory_space=pltpu.SMEM)
NT = (((1,), (1,)), ((), ()))


def shift(array, axis, move):
    peers = lax.axis_size(axis)
    return lax.ppermute(array, axis, [(i, move(i) % peers) for i in range(peers)])


def as_column(row):
    return jnp.broadcast_to(row, (128, row.shape[1])).T[:, 0:1]


def as_row(column):
    return jnp.broadcast_to(column, (column.shape[0], 128)).T[0:1, :]


def log_join(*parts):
    top = functools.reduce(jnp.maximum, parts)
    return top + jnp.log(sum(jnp.exp(part - top) for part in parts))


def flat(entries):
    return [array for entry in entries for array in (entry if isinstance(entry, tuple) else (entry,))]


def like(entries, refs):
    refs = list(refs)
    return [tuple(refs.pop(0) for _ in entry) if isinstance(entry, tuple) else refs.pop(0) for entry in entries]


def fetch(flag, sources, target, sems):
    copies, row = [], 0
    for i, source in enumerate(sources):
        both = source if isinstance(source, tuple) else (source,)
        rows = both[0].shape[0]
        here = [pltpu.make_async_copy(one, target.at[pl.ds(row, rows)], sems.at[i]) for one in both]
        if len(here) == 1:
            here[0].start()
        else:
            pl.when(flag[0] == 1)(here[0].start)
            pl.when(flag[0] != 1)(here[1].start)
        copies.append(here[0])
        row += rows
    return copies


def choose_kernel(flag, first, second, out, sem):
    @pl.when(flag[0] == 1)
    def _():
        pltpu.make_async_copy(first, out, sem).start()

    @pl.when(flag[0] != 1)
    def _():
        pltpu.make_async_copy(second, out, sem).start()

    pltpu.make_async_copy(first, out, sem).wait()


def choose(flag, first, second):
    return pl.pallas_call(
        choose_kernel,
        out_shape=jax.ShapeDtypeStruct(first.shape, first.dtype),
        in_specs=[SCALAR, ANYWHERE, ANYWHERE],
        out_specs=WHOLE,
        scratch_shapes=[pltpu.SemaphoreType.DMA],
        compiler_params=pltpu.CompilerParams(vmem_limit_bytes=VMEM_LIMIT),
        cost_estimate=pl.CostEstimate(flops=0, bytes_accessed=2 * first.size * 2, transcendentals=0),
    )(flag, first, second)


def after(value, *landed):
    return lax.optimization_barrier((value, landed))[0]


def kept(shape, dtype):
    return pltpu.VMEM(shape, dtype)


def in_vmem(array):
    return pltpu.with_memory_space_constraint(array, pltpu.VMEM)


def ids(scalars, which, rows):
    return scalars[which] + lax.broadcasted_iota(jnp.int32, (1, rows), 1)


def side_by_side(first, second):
    return jnp.concatenate([first, second], axis=1)


def score_kernel(form, pairs, early, stats, factor, scalars, *refs):
    mine = refs[:2]
    count = len(flat(form))
    shards = like(form, refs[2 : 2 + count])
    rest = list(refs[2 + count :])
    if stats:
        side = [rest.pop(0) for _ in range(2 if early else 1)]
    out, right = rest.pop(0), rest.pop(0)
    if stats:
        info = rest.pop(0)
    left, sems = rest
    copies = fetch(scalars, mine, left, sems) + fetch(scalars, shards, right, sems.at[pl.ds(2, len(form))])
    for copy in copies[:2]:
        copy.wait()
    rows = mine[0].shape[0]
    pair = 2 * rows
    per_pair = len(form) // pairs
    lhs = left[...]
    row_parts = []
    for p in range(pairs):
        for copy in copies[2 + p * per_pair : 2 + (p + 1) * per_pair]:
            copy.wait()
        s = lax.dot_general(
            lhs, right[pl.ds(p * pair, pair), :], NT, preferred_element_type=F32
        ) * factor
        out[:, pl.ds(p * pair, pair)] = s
        if stats:
            col_max = jnp.max(s, axis=0, keepdims=True)
            col = col_max + jnp.log(jnp.sum(jnp.exp(s - col_max), axis=0, keepdims=True))
            row_max = jnp.max(s, axis=1, keepdims=True)
            row_sum = jnp.sum(jnp.exp(s - row_max), axis=1, keepdims=True)
            row_parts.append(row_max + jnp.log(row_sum))
            info[pl.ds(p if early else 3, 1), :] = col
            if early and p == 0:
                chosen = as_column(side_by_side(side[0][...], side[1][...]))
                hit = chosen == side_by_side(ids(scalars, 1, rows), ids(scalars, 2, rows))
                info[pl.ds(5, 1), :] = as_row(jnp.sum(jnp.where(hit, s, 0.0), axis=1, keepdims=True))
    if stats:
        row = as_row(log_join(*row_parts) if len(row_parts) > 1 else row_parts[0])
        if early:
            info[pl.ds(3, 1), :] = jnp.zeros((1, pair), F32)
            info[pl.ds(4, 1), :] = row
            info[pl.ds(6, 2), :] = jnp.zeros((2, pair), F32)
        else:
            info[pl.ds(0, 3), :] = side[0][pl.ds(0, 3), :]
            info[pl.ds(4, 1), :] = log_join(row, side[0][pl.ds(4, 1), :])
            info[pl.ds(5, 3), :] = side[0][pl.ds(5, 3), :]


def score(scalars, mine, shards, pairs, early, stats, factor, side=()):
    rows, width = mine[0].shape
    tokens = 2 * pairs
    shapes = [kept((2 * rows, tokens * rows), F32), kept((tokens * rows, width), jnp.bfloat16)]
    if stats:
        shapes.append(jax.ShapeDtypeStruct((8, 2 * rows), F32))
    arrays = flat(shards)
    return pl.pallas_call(
        functools.partial(score_kernel, shards, pairs, early, stats, factor),
        out_shape=tuple(shapes),
        in_specs=[SCALAR] + [ANYWHERE] * (2 + len(arrays)) + [WHOLE] * len(side),
        out_specs=(WHOLE,) * len(shapes),
        scratch_shapes=[
            pltpu.VMEM((2 * rows, width), jnp.bfloat16),
            pltpu.SemaphoreType.DMA((2 + len(shards),)),
        ],
        compiler_params=pltpu.CompilerParams(vmem_limit_bytes=VMEM_LIMIT),
        cost_estimate=pl.CostEstimate(
            flops=4 * rows * rows * tokens * width,
            bytes_accessed=(tokens + 2) * rows * width * 2 + 8 * rows * rows * tokens,
            transcendentals=4 * rows * rows * tokens if stats else 0,
        ),
    )(scalars, *mine, *arrays, *side)


def halves(ref, row):
    n = ref.shape[1] // 2
    both = ref[pl.ds(row, 1), :]
    return both[:, :n], both[:, n:]


def by_shard(ref):
    a, b, early, late = (halves(ref, i) for i in range(4))
    return [a[0], a[1], b[0], b[1], early[0], late[0], early[1], late[1]]


def block_kernel(own, across, core, corner, out):
    for base, near, far in ((0, own, across), (8, core, corner)):
        near, far = by_shard(near), by_shard(far)
        for i in range(8):
            out[pl.ds(base + i, 1), :] = log_join(near[i], far[i ^ 1])
    own_row, core_row = halves(own, 4), halves(core, 4)
    across_row, corner_row = halves(across, 4), halves(corner, 4)
    out[pl.ds(16, 1), :] = log_join(own_row[0], core_row[1])
    out[pl.ds(17, 1), :] = log_join(across_row[0], corner_row[1])
    out[pl.ds(18, 1), :] = log_join(own_row[1], core_row[0])
    out[pl.ds(19, 1), :] = halves(own, 5)[0] + halves(core, 5)[1]
    out[pl.ds(20, 4), :] = jnp.zeros((4, out.shape[1]), F32)


def window_kernel(scalars, partner, own, beside, far, ahead, behind, col_out, row_out, loss_out):
    even = scalars[0] == 1
    size = own.shape[0]

    def pick(first, second):
        return jnp.where(even, first, second)

    def line(d, i):
        one = lambda ref, at=0: ref[pl.ds(at + i, 1), :]
        if d == 0:
            return one(own)
        if d in (2, -2):
            return one(ahead if d == 2 else behind)
        if d == 1:
            return pick(one(beside), one(ahead, size))
        if d == -1:
            return pick(one(behind, size), one(beside))
        if d == 3:
            return pick(one(ahead, size), one(far))
        return pick(one(far), one(behind, size))

    def total(step, base, half):
        parts = []
        for other in range(4):
            d = other - step
            if other % 2 == 0:
                parts.append(line(d, base + other + half))
            else:
                c, e = line(d, base + 4 + half), line(d, base + 6 + half)
                c_first = (other == 1) == (d % 2 == 0)
                parts.append(pick(c, e) if c_first else pick(e, c))
        return log_join(*parts)

    sums = [[total(step, 0, half) for half in range(2)] for step in range(4)]
    core_sums = [total(0, 8, half) for half in range(2)]
    c = [pick(sums[1][h], sums[3][h]) for h in range(2)]
    e = [pick(sums[3][h], sums[1][h]) for h in range(2)]
    col_out[pl.ds(0, 1), :] = side_by_side(*sums[0])
    col_out[pl.ds(1, 1), :] = side_by_side(*sums[2])
    col_out[pl.ds(2, 1), :] = side_by_side(c[0], e[0])
    col_out[pl.ds(3, 1), :] = side_by_side(c[1], e[1])
    col_out[pl.ds(4, 1), :] = side_by_side(sums[0][0], core_sums[0])
    near = [line(1, 16 + h) for h in range(2)]
    third = [line(3, 16 + h) for h in range(2)]
    c = [pick(third[h], near[h]) for h in range(2)]
    e = [pick(near[h], third[h]) for h in range(2)]
    row_out[pl.ds(0, 1), :] = side_by_side(line(0, 16), line(0, 17))
    row_out[pl.ds(1, 1), :] = side_by_side(line(2, 16), line(2, 17))
    row_out[pl.ds(2, 1), :] = side_by_side(c[0], e[0])
    row_out[pl.ds(3, 1), :] = side_by_side(c[1], e[1])
    row_out[pl.ds(4, 1), :] = side_by_side(line(0, 16), line(0, 18))
    zeros = jnp.zeros((3, col_out.shape[1]), F32)
    col_out[pl.ds(5, 3), :] = zeros
    row_out[pl.ds(5, 3), :] = zeros
    chosen = as_column(partner[...])
    found = jnp.zeros(chosen.shape, F32)
    for i, value in enumerate((sums[0][0], sums[0][1], core_sums[0], core_sums[1])):
        hit = chosen == ids(scalars, i + 1, value.shape[1])
        found = found + jnp.sum(jnp.where(hit, value, 0.0), axis=1, keepdims=True)
    loss_out[...] = 0.5 * line(0, 16) + 0.5 * as_row(found) - line(0, 19)


def small_call(kernel, shapes, *args, scalars=0):
    return pl.pallas_call(
        kernel,
        out_shape=tuple(jax.ShapeDtypeStruct(s, F32) for s in shapes),
        in_specs=[SCALAR] * scalars + [WHOLE] * (len(args) - scalars),
        out_specs=(WHOLE,) * len(shapes),
        compiler_params=pltpu.CompilerParams(vmem_limit_bytes=VMEM_LIMIT),
        cost_estimate=pl.CostEstimate(flops=100000, bytes_accessed=400000, transcendentals=20000),
    )(*args)


def grad_kernel(form, keys, factor, scalars, early, held_early, row_info, col_info, first, second, *refs):
    rows = first.shape[1]
    pair = 2 * rows
    refs = list(refs)
    if form is None:
        late, held_late = refs.pop(0), refs.pop(0)
    else:
        lhs_parts = [refs.pop(0), refs.pop(0)]
        shards = like(form, [refs.pop(0) for _ in flat(form)])
    own_out, other_out, weights = refs[:3]
    if form is not None:
        held_late, lhs, sems = refs[3:]
        copies = fetch(scalars, lhs_parts, lhs, sems)
        copies += fetch(scalars, shards, held_late, sems.at[pl.ds(2, len(form))])
    row = as_column(row_info[pl.ds(4, 1), :])
    partners = side_by_side(first[...], second[...])
    across = side_by_side(ids(scalars, 1, rows), ids(scalars, 2, rows))
    if keys:
        row_ids, col_ids = as_column(side_by_side(ids(scalars, 1, rows), ids(scalars, 3, rows))), partners
    else:
        row_ids, col_ids = as_column(partners), across
    for p in range(4):
        if p == 3 and form is not None:
            for copy in copies:
                copy.wait()
        for group in (1, 0):
            here = slice(group * rows, (group + 1) * rows)
            there = pl.ds(group * rows, rows)
            if p < 3:
                s = early[there, pl.ds(p * pair, pair)]
            elif form is None:
                s = late[there, :]
            else:
                s = lax.dot_general(
                    lhs[there, :], held_late[...], NT, preferred_element_type=F32
                ) * factor
            w = 0.5 * jnp.exp(s - row[here]) + 0.5 * jnp.exp(s - col_info[pl.ds(p, 1), :])
            if p == 0:
                w = w - jnp.where(row_ids[here] == col_ids, 1.0, 0.0)
            weights[there, pl.ds(p * pair, pair)] = w.astype(jnp.bfloat16)
    for group, out in ((1, other_out), (0, own_out)):
        there = pl.ds(group * rows, rows)
        total = jnp.dot(weights[there, pl.ds(0, 3 * pair)], held_early[...], preferred_element_type=F32)
        total = total + jnp.dot(weights[there, pl.ds(3 * pair, pair)], held_late[...], preferred_element_type=F32)
        out[...] = total * factor


def grad(scalars, keys, factor, early, held_early, row_info, col_info, first, second, late, form=None):
    rows, width = first.shape[1], held_early.shape[1]
    if form is None:
        late = tuple(map(in_vmem, late))
        late_specs, scratch = [WHOLE] * 2, []
    else:
        late = tuple(late) + tuple(flat(form))
        late_specs = [ANYWHERE] * len(late)
        scratch = [
            pltpu.VMEM((2 * rows, width), jnp.bfloat16),
            pltpu.VMEM((2 * rows, width), jnp.bfloat16),
            pltpu.SemaphoreType.DMA((2 + len(form),)),
        ]
    return pl.pallas_call(
        functools.partial(grad_kernel, form, keys, factor),
        out_shape=(jax.ShapeDtypeStruct((rows, width), F32),) * 2,
        in_specs=[SCALAR] + [WHOLE] * 6 + late_specs,
        out_specs=(WHOLE,) * 2,
        scratch_shapes=[pltpu.VMEM((2 * rows, 8 * rows), jnp.bfloat16)] + scratch,
        compiler_params=pltpu.CompilerParams(vmem_limit_bytes=VMEM_LIMIT),
        cost_estimate=pl.CostEstimate(
            flops=32 * rows * rows * width,
            bytes_accessed=8 * rows * width * 2 + 64 * rows * rows + rows * width * 8,
            transcendentals=32 * rows * rows,
        ),
    )(scalars, in_vmem(early), in_vmem(held_early), row_info, col_info, first, second, *late)


def local(query_rows, key_rows, partner):
    rows, features = query_rows.shape
    factor = float(features) ** (-0.5)
    block = lax.axis_index("blk")
    place = lax.axis_index("pb")
    even = block % 2 == 0
    starts = [(place ^ other) * rows for other in (0, 2, 1, 3)]
    scalars = jnp.stack([even.astype(jnp.int32), *starts])
    pick = functools.partial(choose, scalars)

    across = lambda a: shift(a, PART_AXIS, lambda i: i ^ 2)
    core = lambda a: shift(a, PART_AXIS, lambda i: i ^ 1)
    corner = lambda a: shift(a, PART_AXIS, lambda i: i ^ 3)
    beside = lambda a: shift(a, BLOCK_AXIS, lambda i: i ^ 1)
    ahead = lambda a: shift(a, BLOCK_AXIS, lambda i: i + 2)
    back = lambda a: shift(a, BLOCK_AXIS, lambda i: i - 2)
    apart = lambda a: shift(a, BLOCK_AXIS, lambda i: i + 2 if i % 2 == 0 else i - 2)

    k0, q0 = key_rows, query_rows
    y1_in = pick(k0, q0)
    y1, kz, kx = beside(y1_in), ahead(after(k0, y1_in)), across(after(k0, y1_in))
    ks, qs = core(k0), core(q0)
    partner_core = core(partner)

    qx = across(after(q0, kx))
    kzy = beside(after(kz, y1))
    qz = back(after(q0, kz))

    kzx = across(after(kz, qx))
    qzy = beside(after(qz, kzy))
    m1 = apart(after(pick(kzy, qx), qz))

    kd0 = pick(m1, y1)
    kd1 = across(after(kd0, kzx))
    kzxy = beside(after(kzx, qzy))
    m2 = back(after(pick(qx, qzy), m1))
    qd0, qzx = pick(y1, m2), pick(m2, m1)

    k_shards = (k0, kx, kz, kzx, kzy, kd0, kzxy, kd1)
    s_early, k_early, info = score(
        scalars, (q0, qs), k_shards[:6], 3, True, True, factor, (partner, partner_core)
    )
    x_cut, y_cut = CUTS
    qd1_0 = across(after(qd0[:x_cut], kd1, info))
    qzxy_0 = beside(after(qzx[:y_cut], kzxy, info))
    s_late, k_late, info = score(scalars, (q0, qs), k_shards[6:], 1, False, True, factor, (info,))
    info = after(info, qd1_0)
    own = small_call(block_kernel, [(24, rows)], info, across(info), core(info), corner(info))[0]
    qd1_1 = across(after(qd0[x_cut:], own))
    own = after(own, qzxy_0)
    next_to = beside(own)
    far = shift(own, BLOCK_AXIS, lambda i: i - 3 if i % 2 == 0 else i + 3)
    both = jnp.concatenate([own, next_to], axis=0)
    col_info, row_info, loss = small_call(
        window_kernel,
        [(8, 2 * rows), (8, 2 * rows), (1, rows)],
        scalars, partner, own, next_to, far, back(both), ahead(both),
        scalars=1,
    )
    qzxy_1 = beside(after(qzx[y_cut:], next_to))
    partner_across = across(after(partner, own))
    t_early, q_early = score(
        scalars, (after(k0, next_to), ks), (q0, qx, qz, qzx, qzy, qd0), 3, True, False, factor
    )
    q_own, q_other = grad(
        scalars, False, factor, s_early, k_early, row_info, col_info, partner, partner_core, (s_late, k_late)
    )
    k_own, k_other = grad(
        scalars, True, factor, t_early, q_early, col_info, row_info, partner, partner_across,
        (k0, ks), (qzxy_0, qzxy_1, qd1_0, qd1_1),
    )
    grad_queries = q_own + core(q_other)
    grad_keys = k_own + core(k_other)
    return (loss[0], grad_queries, grad_keys)


def solution(mesh):
    return jax.shard_map(
        local,
        mesh=mesh,
        in_specs=(P(("blk", "pb"), None), P(("blk", "pb"), None), P("blk", "pb")),
        out_specs=(P(("blk", "pb")), P(("blk", "pb"), None), P(("blk", "pb"), None)),
        check_vma=False,
    )
```

```python
import functools

import jax
import jax.numpy as jnp
from jax import lax
from jax.experimental import pallas as pl
from jax.experimental.pallas import tpu as pltpu
from jax.sharding import PartitionSpec as P

F32 = jnp.float32
BLOCK_AXIS, PART_AXIS = "blk", "pb"
VMEM_LIMIT = 16 * 1024 * 1024
ANYWHERE = pl.BlockSpec(memory_space=pl.ANY)
WHOLE = pl.BlockSpec(memory_space=pltpu.VMEM)
SCALAR = pl.BlockSpec(memory_space=pltpu.SMEM)
NT = (((1,), (1,)), ((), ()))


def shift(array, axis, move, among=None):
    peers = lax.axis_size(axis)
    pairs = [(i, move(i) % peers) for i in range(peers) if among is None or among(i)]
    return lax.ppermute(array, axis, pairs)


def as_column(row):
    return jnp.broadcast_to(row, (128, row.shape[1])).T[:, 0:1]


def as_row(column):
    return jnp.broadcast_to(column, (column.shape[0], 128)).T[0:1, :]


def log_join(*parts):
    top = functools.reduce(jnp.maximum, parts)
    return top + jnp.log(sum(jnp.exp(part - top) for part in parts))


def fetch(sources, target, sems):
    copies, row = [], 0
    for i, source in enumerate(sources):
        rows = source.shape[0]
        copy = pltpu.make_async_copy(source, target.at[pl.ds(row, rows)], sems.at[i])
        copy.start()
        copies.append(copy)
        row += rows
    return copies


def choose_kernel(flag, first, second, out, sem):
    @pl.when(flag[0] == 1)
    def _():
        pltpu.make_async_copy(first, out, sem).start()

    @pl.when(flag[0] != 1)
    def _():
        pltpu.make_async_copy(second, out, sem).start()

    pltpu.make_async_copy(first, out, sem).wait()


def choose(flag, first, second):
    return pl.pallas_call(
        choose_kernel,
        out_shape=jax.ShapeDtypeStruct(first.shape, first.dtype),
        in_specs=[SCALAR, ANYWHERE, ANYWHERE],
        out_specs=WHOLE,
        scratch_shapes=[pltpu.SemaphoreType.DMA],
        compiler_params=pltpu.CompilerParams(vmem_limit_bytes=VMEM_LIMIT),
        cost_estimate=pl.CostEstimate(flops=0, bytes_accessed=2 * first.size * 2, transcendentals=0),
    )(flag, first, second)


def after(value, *landed):
    return lax.optimization_barrier((value, landed))[0]


def kept(shape, dtype):
    return pltpu.VMEM(shape, dtype)


def in_vmem(array):
    return pltpu.with_memory_space_constraint(array, pltpu.VMEM)


def ids(scalars, which, rows):
    return scalars[which] + lax.broadcasted_iota(jnp.int32, (1, rows), 1)


def side_by_side(first, second):
    return jnp.concatenate([first, second], axis=1)


def score_kernel(count, start, stats, factor, scalars, *refs):
    mine = refs[:2]
    shards = refs[2 : 2 + count]
    rest = list(refs[2 + count :])
    *side, out, right, info, left, sems = rest
    copies = fetch(mine, left, sems) + fetch(shards, right, sems.at[pl.ds(2, count)])
    for copy in copies[:2]:
        copy.wait()
    rows = mine[0].shape[0]
    pair = 2 * rows
    lhs = left[...]
    row_parts = []
    if not stats:
        info[...] = jnp.zeros(info.shape, F32)
    elif start:
        info[...] = side[0][...]
    waiting = copies[2:]
    ends = [sum(shard.shape[0] for shard in shards[: i + 1]) for i in range(count)]
    for p in range(ends[-1] // pair):
        while waiting and ends[-len(waiting)] - shards[-len(waiting)].shape[0] < (p + 1) * pair:
            waiting.pop(0).wait()
        s = lax.dot_general(
            lhs, right[pl.ds(p * pair, pair), :], NT, preferred_element_type=F32
        ) * factor
        out[:, pl.ds(p * pair, pair)] = s
        if stats:
            col_max = jnp.max(s, axis=0, keepdims=True)
            col = col_max + jnp.log(jnp.sum(jnp.exp(s - col_max), axis=0, keepdims=True))
            row_max = jnp.max(s, axis=1, keepdims=True)
            row_sum = jnp.sum(jnp.exp(s - row_max), axis=1, keepdims=True)
            row_parts.append(row_max + jnp.log(row_sum))
            info[pl.ds(start + p, 1), :] = col
            if start + p == 0:
                chosen = as_column(side_by_side(side[0][...], side[1][...]))
                hit = chosen == side_by_side(ids(scalars, 1, rows), ids(scalars, 2, rows))
                info[pl.ds(5, 1), :] = as_row(jnp.sum(jnp.where(hit, s, 0.0), axis=1, keepdims=True))
    if stats:
        row = as_row(log_join(*row_parts) if len(row_parts) > 1 else row_parts[0])
        if start:
            row = log_join(row, side[0][pl.ds(4, 1), :])
        else:
            info[pl.ds(2, 2), :] = jnp.zeros((2, pair), F32)
            info[pl.ds(6, 2), :] = jnp.zeros((2, pair), F32)
        info[pl.ds(4, 1), :] = row


def score(scalars, mine, shards, start, stats, factor, side=()):
    rows, width = mine[0].shape
    tokens = sum(shard.shape[0] for shard in shards) // rows
    info = (8, 2 * rows) if stats else (8, 128)
    shapes = [
        kept((2 * rows, tokens * rows), F32),
        kept((tokens * rows, width), jnp.bfloat16),
        jax.ShapeDtypeStruct(info, F32),
    ]
    return pl.pallas_call(
        functools.partial(score_kernel, len(shards), start, stats, factor),
        out_shape=tuple(shapes),
        in_specs=[SCALAR] + [ANYWHERE] * (2 + len(shards)) + [WHOLE] * len(side),
        out_specs=(WHOLE,) * len(shapes),
        scratch_shapes=[
            pltpu.VMEM((2 * rows, width), jnp.bfloat16),
            pltpu.SemaphoreType.DMA((2 + len(shards),)),
        ],
        compiler_params=pltpu.CompilerParams(vmem_limit_bytes=VMEM_LIMIT),
        cost_estimate=pl.CostEstimate(
            flops=4 * rows * rows * tokens * width,
            bytes_accessed=(tokens + 2) * rows * width * 2 + 8 * rows * rows * tokens,
            transcendentals=4 * rows * rows * tokens if stats else 0,
        ),
    )(scalars, *mine, *shards, *side)


def halves(line):
    n = line.shape[1] // 2
    return line[:, :n], line[:, n:]


def by_shard(lines):
    p = [halves(line) for line in lines]
    return [p[0][0], p[0][1], p[1][0], p[2][0], p[1][1], p[3][0], p[2][1], p[3][1]]


def chain_kernel(scalars, own, beside, far, ahead, behind, out):
    even = scalars[0] == 1
    size = own.shape[0]

    def pick(first, second):
        return jnp.where(even, first, second)

    def line(d, i):
        one = lambda ref, at=0: ref[pl.ds(at + i, 1), :]
        if d == 0:
            return one(own)
        if d in (2, -2):
            return one(ahead if d == 2 else behind)
        if d == 1:
            return pick(one(beside), one(ahead, size))
        if d == -1:
            return pick(one(behind, size), one(beside))
        if d == 3:
            return pick(one(ahead, size), one(far))
        return pick(one(far), one(behind, size))

    shards = {d: by_shard([line(d, i) for i in range(4)]) for d in range(-3, 4)}

    def total(step, half):
        parts = []
        for other in range(4):
            d = other - step
            if other % 2 == 0:
                parts.append(shards[d][other + half])
            else:
                c, e = shards[d][4 + half], shards[d][6 + half]
                c_first = (other == 1) == (d % 2 == 0)
                parts.append(pick(c, e) if c_first else pick(e, c))
        return log_join(*parts)

    sums = [[total(step, half) for half in range(2)] for step in range(4)]
    for half in range(2):
        out[pl.ds(half, 1), :] = sums[0][half]
        out[pl.ds(2 + half, 1), :] = sums[2][half]
        out[pl.ds(4 + half, 1), :] = pick(sums[1][half], sums[3][half])
        out[pl.ds(6 + half, 1), :] = pick(sums[3][half], sums[1][half])
    row = {d: halves(line(d, 4)) for d in range(4)}
    for half in range(2):
        at = 8 + 4 * half
        out[pl.ds(at, 1), :] = row[0][half]
        out[pl.ds(at + 1, 1), :] = row[2][half]
        out[pl.ds(at + 2, 1), :] = pick(row[3][half], row[1][half])
        out[pl.ds(at + 3, 1), :] = pick(row[1][half], row[3][half])
    positive = halves(line(0, 5))
    out[pl.ds(16, 1), :] = positive[0]
    out[pl.ds(17, 1), :] = positive[1]
    out[pl.ds(18, 6), :] = jnp.zeros((6, out.shape[1]), F32)


def block_kernel(scalars, partner, own, across, core, corner, col_out, row_out, loss_out):
    line = lambda ref, i: ref[pl.ds(i, 1), :]
    col = [[log_join(line(own, 2 * i + h), line(across, 2 * i + 1 - h)) for h in range(2)] for i in range(4)]
    core_col = [log_join(line(core, h), line(corner, 1 - h)) for h in range(2)]
    row = [
        [log_join(line(own, 8 + i), line(core, 12 + i)), log_join(line(across, 8 + i), line(corner, 12 + i))]
        for i in range(4)
    ]
    core_row = log_join(line(own, 12), line(core, 8))
    zeros = jnp.zeros((3, col_out.shape[1]), F32)
    for out, part, more in ((col_out, col, core_col[0]), (row_out, row, core_row)):
        a, b, c, d = part
        out[pl.ds(0, 1), :] = side_by_side(a[0], a[1])
        out[pl.ds(1, 1), :] = side_by_side(b[0], c[0])
        out[pl.ds(2, 1), :] = side_by_side(b[1], d[0])
        out[pl.ds(3, 1), :] = side_by_side(c[1], d[1])
        out[pl.ds(4, 1), :] = side_by_side(a[0], more)
        out[pl.ds(5, 3), :] = zeros
    chosen = as_column(partner[...])
    found = jnp.zeros(chosen.shape, F32)
    for i, value in enumerate((col[0][0], col[0][1], core_col[0], core_col[1])):
        hit = chosen == ids(scalars, i + 1, value.shape[1])
        found = found + jnp.sum(jnp.where(hit, value, 0.0), axis=1, keepdims=True)
    score = line(own, 16) + line(core, 17)
    loss_out[...] = (0.5 * row[0][0] + 0.5 * as_row(found) - score)[0]


def small_call(kernel, shapes, *args, scalars=0):
    return pl.pallas_call(
        kernel,
        out_shape=tuple(jax.ShapeDtypeStruct(s, F32) for s in shapes),
        in_specs=[SCALAR] * scalars + [WHOLE] * (len(args) - scalars),
        out_specs=(WHOLE,) * len(shapes),
        compiler_params=pltpu.CompilerParams(vmem_limit_bytes=VMEM_LIMIT),
        cost_estimate=pl.CostEstimate(flops=100000, bytes_accessed=400000, transcendentals=20000),
    )(*args)


def grad_kernel(keys, factor, scalars, first, second, row_info, col_info, *refs):
    rows = first.shape[1]
    pair = 2 * rows
    *made, own_out, other_out, weights = refs
    made = list(zip(made[::2], made[1::2]))
    row = as_column(row_info[pl.ds(4, 1), :])
    partners = side_by_side(first[...], second[...])
    across = side_by_side(ids(scalars, 1, rows), ids(scalars, 2, rows))
    if keys:
        row_ids, col_ids = as_column(side_by_side(ids(scalars, 1, rows), ids(scalars, 3, rows))), partners
    else:
        row_ids, col_ids = as_column(partners), across

    def weigh(p, group, s):
        here = slice(group * rows, (group + 1) * rows)
        w = 0.5 * jnp.exp(s - row[here]) + 0.5 * jnp.exp(s - col_info[pl.ds(p, 1), :])
        if p == 0:
            w = w - jnp.where(row_ids[here] == col_ids, 1.0, 0.0)
        weights[pl.ds(group * rows, rows), pl.ds(p * pair, pair)] = w.astype(jnp.bfloat16)

    p = 0
    for scores, _ in made:
        for at in range(0, scores.shape[1], pair):
            for group in (1, 0):
                weigh(p, group, scores[pl.ds(group * rows, rows), pl.ds(at, pair)])
            p += 1
    for group, out in ((1, other_out), (0, own_out)):
        there = pl.ds(group * rows, rows)
        total, at = None, 0
        for _, held in made:
            span = held.shape[0]
            part = jnp.dot(weights[there, pl.ds(at, span)], held[...], preferred_element_type=F32)
            total = part if total is None else total + part
            at += span
        out[...] = total * factor


def grad(scalars, keys, factor, first, second, row_info, col_info, made):
    rows, width = first.shape[1], made[0][1].shape[1]
    made = [in_vmem(array) for part in made for array in part]
    return pl.pallas_call(
        functools.partial(grad_kernel, keys, factor),
        out_shape=(kept((rows, width), F32), kept((rows, width), F32)),
        in_specs=[SCALAR] + [WHOLE] * (4 + len(made)),
        out_specs=(WHOLE,) * 2,
        scratch_shapes=[pltpu.VMEM((2 * rows, 8 * rows), jnp.bfloat16)],
        compiler_params=pltpu.CompilerParams(vmem_limit_bytes=VMEM_LIMIT),
        cost_estimate=pl.CostEstimate(
            flops=32 * rows * rows * width,
            bytes_accessed=8 * rows * width * 2 + 64 * rows * rows + rows * width * 8,
            transcendentals=32 * rows * rows,
        ),
    )(scalars, first, second, row_info, col_info, *made)


def add_kernel(own, received, out, total, sems):
    parts = sems.shape[0]
    step = own.shape[0] // parts
    writes = []
    for i in range(parts):
        here = pl.ds(i * step, step)
        total[here, :] = own[here, :] + received[here, :]
        writes.append(pltpu.make_async_copy(total.at[here], out.at[here], sems.at[i]))
        writes[-1].start()
    for write in writes:
        write.wait()


def add(own, received):
    return pl.pallas_call(
        add_kernel,
        out_shape=jax.ShapeDtypeStruct(own.shape, F32),
        in_specs=[WHOLE] * 2,
        out_specs=ANYWHERE,
        scratch_shapes=[pltpu.VMEM(own.shape, F32), pltpu.SemaphoreType.DMA((4,))],
        compiler_params=pltpu.CompilerParams(vmem_limit_bytes=VMEM_LIMIT),
        cost_estimate=pl.CostEstimate(flops=own.size, bytes_accessed=12 * own.size, transcendentals=0),
    )(in_vmem(own), in_vmem(received))


def local(query_rows, key_rows, partner):
    rows, features = query_rows.shape
    factor = float(features) ** (-0.5)
    block = lax.axis_index("blk")
    place = lax.axis_index("pb")
    even = block % 2 == 0
    starts = [(place ^ other) * rows for other in (0, 2, 1, 3)]
    scalars = jnp.stack([even.astype(jnp.int32), *starts])
    pick = functools.partial(choose, scalars)

    across = lambda a: shift(a, PART_AXIS, lambda i: i ^ 2)
    core = lambda a: shift(a, PART_AXIS, lambda i: i ^ 1)
    corner = lambda a: shift(a, PART_AXIS, lambda i: i ^ 3)
    beside = lambda a, among=None: shift(a, BLOCK_AXIS, lambda i: i ^ 1, among)
    ahead = lambda a: shift(a, BLOCK_AXIS, lambda i: i + 2)
    back = lambda a: shift(a, BLOCK_AXIS, lambda i: i - 2)
    apart = lambda a: shift(a, BLOCK_AXIS, lambda i: i + 2 if i % 2 == 0 else i - 2)

    k0, q0 = key_rows, query_rows
    kz, partner_core, partner_across = ahead(k0), core(partner), across(partner)
    kx = across(after(k0, partner_across))
    y1_odd = beside(after(k0, partner_core), lambda i: i % 2 == 0)
    y1_even = beside(after(q0, partner_core), lambda i: i % 2 == 1)
    ks, qs = core(k0), core(q0)

    qx = across(after(q0, kx))
    kzy = beside(after(kz, y1_odd, y1_even))
    qz = back(after(q0, kz))

    kzx = across(after(kz, qx))
    qzy = beside(after(qz, kzy))
    m1 = apart(after(pick(kzy, qx), qz))

    kd0 = pick(m1, y1_odd)
    kzxy = beside(after(kzx, qzy))
    m2 = back(after(pick(qx, qzy), m1))
    qd0, qzx = pick(y1_even, m2), pick(m2, m1)

    mine = (q0, qs)
    *k_made_0, info = score(scalars, mine, (k0, kx, kz, kzy), 0, True, factor, (partner, partner_core))
    *q_made_0, tick = score(scalars, (k0, ks), (q0, qx, qz, qzy), 0, False, factor, (partner_across,))
    kd1 = across(after(kd0, kzx, info))
    *k_made_1, info = score(scalars, mine, (kzx, kd0), 2, True, factor, (info, tick))
    qd1 = across(after(qd0, info))
    *k_made_2, info = score(scalars, mine, (kzxy, kd1), 3, True, factor, (info,))

    next_to = beside(info)
    far = shift(info, BLOCK_AXIS, lambda i: i - 3 if i % 2 == 0 else i + 3)
    both = jnp.concatenate([info, next_to], axis=0)
    chain = small_call(chain_kernel, [(24, rows)], scalars, info, next_to, far, back(both), ahead(both), scalars=1)[0]
    *q_made_1, tick = score(scalars, (after(k0, next_to), ks), (qzx, qd0), 2, False, factor)
    qzxy = beside(after(qzx, next_to))
    chain = after(chain, qd1)
    col_info, row_info, loss = small_call(
        block_kernel,
        [(8, 2 * rows), (8, 2 * rows), (rows,)],
        scalars, partner, chain, across(chain), core(chain), corner(chain),
        scalars=1,
    )
    *q_made_2, _ = score(scalars, (k0, ks), (qzxy, qd1), 3, False, factor)
    q_own, q_other = grad(
        scalars, False, factor, partner, partner_core, row_info, col_info, (k_made_0, k_made_1, k_made_2)
    )
    k_own, k_other = grad(
        scalars, True, factor, partner, partner_across, col_info, row_info, (q_made_0, q_made_1, q_made_2)
    )
    grad_queries = add(q_own, core(q_other))
    grad_keys = add(k_own, core(k_other))
    return (loss, grad_queries, grad_keys)


def solution(mesh):
    return jax.shard_map(
        local,
        mesh=mesh,
        in_specs=(P(("blk", "pb"), None), P(("blk", "pb"), None), P("blk", "pb")),
        out_specs=(P(("blk", "pb")), P(("blk", "pb"), None), P(("blk", "pb"), None)),
        check_vma=False,
    )
```

```python
import functools

import jax
import jax.numpy as jnp
from jax import lax
from jax.experimental import pallas as pl
from jax.experimental.pallas import tpu as pltpu
from jax.sharding import PartitionSpec as P

F32 = jnp.float32
BLOCK_AXIS, PART_AXIS = "blk", "pb"
VMEM_LIMIT = 16 * 1024 * 1024
ANYWHERE = pl.BlockSpec(memory_space=pl.ANY)
WHOLE = pl.BlockSpec(memory_space=pltpu.VMEM)
SCALAR = pl.BlockSpec(memory_space=pltpu.SMEM)
NT = (((1,), (1,)), ((), ()))


def shift(array, axis, move, among=None):
    peers = lax.axis_size(axis)
    pairs = [(i, move(i) % peers) for i in range(peers) if among is None or among(i)]
    return lax.ppermute(array, axis, pairs)


def as_column(row):
    return jnp.broadcast_to(row, (128, row.shape[1])).T[:, 0:1]


def as_row(column):
    return jnp.broadcast_to(column, (column.shape[0], 128)).T[0:1, :]


def log_join(*parts):
    top = functools.reduce(jnp.maximum, parts)
    return top + jnp.log(sum(jnp.exp(part - top) for part in parts))


def fetch(sources, target, sems):
    copies, row = [], 0
    for i, source in enumerate(sources):
        rows = source.shape[0]
        copy = pltpu.make_async_copy(source, target.at[pl.ds(row, rows)], sems.at[i])
        copy.start()
        copies.append(copy)
        row += rows
    return copies


def choose_kernel(flag, first, second, out, sem):
    @pl.when(flag[0] == 1)
    def _():
        pltpu.make_async_copy(first, out, sem).start()

    @pl.when(flag[0] != 1)
    def _():
        pltpu.make_async_copy(second, out, sem).start()

    pltpu.make_async_copy(first, out, sem).wait()


def choose(flag, first, second):
    return pl.pallas_call(
        choose_kernel,
        out_shape=jax.ShapeDtypeStruct(first.shape, first.dtype),
        in_specs=[SCALAR, ANYWHERE, ANYWHERE],
        out_specs=WHOLE,
        scratch_shapes=[pltpu.SemaphoreType.DMA],
        compiler_params=pltpu.CompilerParams(vmem_limit_bytes=VMEM_LIMIT),
        cost_estimate=pl.CostEstimate(flops=0, bytes_accessed=2 * first.size * 2, transcendentals=0),
    )(flag, first, second)


def after(value, *landed):
    return lax.optimization_barrier((value, landed))[0]


def kept(shape, dtype):
    return pltpu.VMEM(shape, dtype)


def in_vmem(array):
    return pltpu.with_memory_space_constraint(array, pltpu.VMEM)


def ids(scalars, which, rows):
    return scalars[which] + lax.broadcasted_iota(jnp.int32, (1, rows), 1)


def side_by_side(first, second):
    return jnp.concatenate([first, second], axis=1)


def score_kernel(count, given, start, stats, factor, scalars, *refs):
    refs = list(refs)
    mine = refs.pop(0) if given else (refs.pop(0), refs.pop(0))
    shards = [refs.pop(0) for _ in range(count)]
    if given:
        *side, out, right, info, sems = refs
        left = mine
    else:
        *side, out, right, info, left, sems = refs
    copies = fetch(shards, right, sems.at[pl.ds(2, count)])
    if not given:
        for copy in fetch(mine, left, sems):
            copy.wait()
    pair = left.shape[0]
    rows = pair // 2
    lhs = left[...]
    row_parts = []
    if not stats:
        info[...] = jnp.zeros(info.shape, F32)
    elif start:
        info[...] = side[0][...]
    waiting = copies
    ends = [sum(shard.shape[0] for shard in shards[: i + 1]) for i in range(count)]
    for p in range(ends[-1] // pair):
        while waiting and ends[-len(waiting)] - shards[-len(waiting)].shape[0] < (p + 1) * pair:
            waiting.pop(0).wait()
        s = lax.dot_general(
            lhs, right[pl.ds(p * pair, pair), :], NT, preferred_element_type=F32
        ) * factor
        out[:, pl.ds(p * pair, pair)] = s
        if stats:
            col_max = jnp.max(s, axis=0, keepdims=True)
            col = col_max + jnp.log(jnp.sum(jnp.exp(s - col_max), axis=0, keepdims=True))
            row_max = jnp.max(s, axis=1, keepdims=True)
            row_sum = jnp.sum(jnp.exp(s - row_max), axis=1, keepdims=True)
            row_parts.append(row_max + jnp.log(row_sum))
            info[pl.ds(start + p, 1), :] = col
            if start + p == 0:
                chosen = as_column(side_by_side(side[0][...], side[1][...]))
                hit = chosen == side_by_side(ids(scalars, 1, rows), ids(scalars, 2, rows))
                info[pl.ds(5, 1), :] = as_row(jnp.sum(jnp.where(hit, s, 0.0), axis=1, keepdims=True))
    if stats:
        row = as_row(log_join(*row_parts) if len(row_parts) > 1 else row_parts[0])
        if start:
            row = log_join(row, side[0][pl.ds(4, 1), :])
        else:
            info[pl.ds(2, 2), :] = jnp.zeros((2, pair), F32)
            info[pl.ds(6, 2), :] = jnp.zeros((2, pair), F32)
        info[pl.ds(4, 1), :] = row


def score(scalars, mine, shards, start, stats, factor, side=(), keep=False):
    given = not isinstance(mine, tuple)
    width = shards[0].shape[1]
    rows = mine.shape[0] // 2 if given else mine[0].shape[0]
    tokens = sum(shard.shape[0] for shard in shards) // rows
    info = (8, 2 * rows) if stats else (8, 128)
    shapes = [
        kept((2 * rows, tokens * rows), F32),
        kept((tokens * rows, width), jnp.bfloat16),
        jax.ShapeDtypeStruct(info, F32),
    ]
    left = (2 * rows, width)
    if keep:
        shapes.append(kept(left, jnp.bfloat16))
    lhs, lhs_specs = ([in_vmem(mine)], [WHOLE]) if given else (mine, [ANYWHERE] * 2)
    return pl.pallas_call(
        functools.partial(score_kernel, len(shards), given, start, stats, factor),
        out_shape=tuple(shapes),
        in_specs=[SCALAR] + lhs_specs + [ANYWHERE] * len(shards) + [WHOLE] * len(side),
        out_specs=(WHOLE,) * len(shapes),
        scratch_shapes=([] if given or keep else [pltpu.VMEM(left, jnp.bfloat16)])
        + [pltpu.SemaphoreType.DMA((2 + len(shards),))],
        compiler_params=pltpu.CompilerParams(vmem_limit_bytes=VMEM_LIMIT),
        cost_estimate=pl.CostEstimate(
            flops=4 * rows * rows * tokens * width,
            bytes_accessed=(tokens + 2) * rows * width * 2 + 8 * rows * rows * tokens,
            transcendentals=4 * rows * rows * tokens if stats else 0,
        ),
    )(scalars, *lhs, *shards, *side)


def halves(line):
    n = line.shape[1] // 2
    return line[:, :n], line[:, n:]


def by_shard(lines):
    p = [halves(line) for line in lines]
    return [p[0][0], p[0][1], p[1][0], p[2][0], p[1][1], p[3][0], p[2][1], p[3][1]]


def chain_kernel(scalars, own, beside, far, ahead, behind, out):
    even = scalars[0] == 1
    size = own.shape[0]

    def pick(first, second):
        return jnp.where(even, first, second)

    def line(d, i):
        one = lambda ref, at=0: ref[pl.ds(at + i, 1), :]
        if d == 0:
            return one(own)
        if d in (2, -2):
            return one(ahead if d == 2 else behind)
        if d == 1:
            return pick(one(beside), one(ahead, size))
        if d == -1:
            return pick(one(behind, size), one(beside))
        if d == 3:
            return pick(one(ahead, size), one(far))
        return pick(one(far), one(behind, size))

    shards = {d: by_shard([line(d, i) for i in range(4)]) for d in range(-3, 4)}

    def total(step, half):
        parts = []
        for other in range(4):
            d = other - step
            if other % 2 == 0:
                parts.append(shards[d][other + half])
            else:
                c, e = shards[d][4 + half], shards[d][6 + half]
                c_first = (other == 1) == (d % 2 == 0)
                parts.append(pick(c, e) if c_first else pick(e, c))
        return log_join(*parts)

    sums = [[total(step, half) for half in range(2)] for step in range(4)]
    for half in range(2):
        out[pl.ds(half, 1), :] = sums[0][half]
        out[pl.ds(2 + half, 1), :] = sums[2][half]
        out[pl.ds(4 + half, 1), :] = pick(sums[1][half], sums[3][half])
        out[pl.ds(6 + half, 1), :] = pick(sums[3][half], sums[1][half])
    row = {d: halves(line(d, 4)) for d in range(4)}
    for half in range(2):
        at = 8 + 4 * half
        out[pl.ds(at, 1), :] = row[0][half]
        out[pl.ds(at + 1, 1), :] = row[2][half]
        out[pl.ds(at + 2, 1), :] = pick(row[3][half], row[1][half])
        out[pl.ds(at + 3, 1), :] = pick(row[1][half], row[3][half])
    positive = halves(line(0, 5))
    out[pl.ds(16, 1), :] = positive[0]
    out[pl.ds(17, 1), :] = positive[1]
    out[pl.ds(18, 6), :] = jnp.zeros((6, out.shape[1]), F32)


def block_sums(own, across, core, corner):
    line = lambda ref, i: ref[pl.ds(i, 1), :]
    col = [[log_join(line(own, 2 * i + h), line(across, 2 * i + 1 - h)) for h in range(2)] for i in range(4)]
    core_col = [log_join(line(core, h), line(corner, 1 - h)) for h in range(2)]
    row = [
        [log_join(line(own, 8 + i), line(core, 12 + i)), log_join(line(across, 8 + i), line(corner, 12 + i))]
        for i in range(4)
    ]
    core_row = log_join(line(own, 12), line(core, 8))
    return col, core_col, row, core_row


def fill_info(sums, col_out, row_out):
    col, core_col, row, core_row = sums
    zeros = jnp.zeros((3, col_out.shape[1]), F32)
    for out, part, more in ((col_out, col, core_col[0]), (row_out, row, core_row)):
        a, b, c, d = part
        out[pl.ds(0, 1), :] = side_by_side(a[0], a[1])
        out[pl.ds(1, 1), :] = side_by_side(b[0], c[0])
        out[pl.ds(2, 1), :] = side_by_side(b[1], d[0])
        out[pl.ds(3, 1), :] = side_by_side(c[1], d[1])
        out[pl.ds(4, 1), :] = side_by_side(a[0], more)
        out[pl.ds(5, 3), :] = zeros


def loss_kernel(scalars, partner, own, across, core, corner, out):
    col, core_col, row, _ = block_sums(own, across, core, corner)
    chosen = as_column(partner[...])
    found = jnp.zeros(chosen.shape, F32)
    for i, value in enumerate((col[0][0], col[0][1], core_col[0], core_col[1])):
        hit = chosen == ids(scalars, i + 1, value.shape[1])
        found = found + jnp.sum(jnp.where(hit, value, 0.0), axis=1, keepdims=True)
    score = own[pl.ds(16, 1), :] + core[pl.ds(17, 1), :]
    out[...] = (0.5 * row[0][0] + 0.5 * as_row(found) - score)[0]


def small_call(kernel, shapes, *args, scalars=0):
    return pl.pallas_call(
        kernel,
        out_shape=tuple(jax.ShapeDtypeStruct(s, F32) for s in shapes),
        in_specs=[SCALAR] * scalars + [WHOLE] * (len(args) - scalars),
        out_specs=(WHOLE,) * len(shapes),
        compiler_params=pltpu.CompilerParams(vmem_limit_bytes=VMEM_LIMIT),
        cost_estimate=pl.CostEstimate(flops=100000, bytes_accessed=400000, transcendentals=20000),
    )(*args)


def grad_kernel(keys, factor, scalars, first, second, *refs):
    rows = first.shape[1]
    pair = 2 * rows
    if keys:
        row_info, col_info, *made, own_out, other_out, weights = refs
    else:
        *made, own_out, other_out, col_info, row_info, weights = refs[4:]
        fill_info(block_sums(*refs[:4]), col_info, row_info)
    made = list(zip(made[::2], made[1::2]))
    row = as_column(row_info[pl.ds(4, 1), :])
    partners = side_by_side(first[...], second[...])
    across = side_by_side(ids(scalars, 1, rows), ids(scalars, 2, rows))
    if keys:
        row_ids, col_ids = as_column(side_by_side(ids(scalars, 1, rows), ids(scalars, 3, rows))), partners
    else:
        row_ids, col_ids = as_column(partners), across

    def weigh(p, group, s):
        here = slice(group * rows, (group + 1) * rows)
        w = 0.5 * jnp.exp(s - row[here]) + 0.5 * jnp.exp(s - col_info[pl.ds(p, 1), :])
        if p == 0:
            w = w - jnp.where(row_ids[here] == col_ids, 1.0, 0.0)
        weights[pl.ds(group * rows, rows), pl.ds(p * pair, pair)] = w.astype(jnp.bfloat16)

    p = 0
    for scores, _ in made:
        for at in range(0, scores.shape[1], pair):
            for group in (1, 0):
                weigh(p, group, scores[pl.ds(group * rows, rows), pl.ds(at, pair)])
            p += 1
    for group, out in ((1, other_out), (0, own_out)):
        there = pl.ds(group * rows, rows)
        total, at = None, 0
        for _, held in made:
            span = held.shape[0]
            part = jnp.dot(weights[there, pl.ds(at, span)], held[...], preferred_element_type=F32)
            total = part if total is None else total + part
            at += span
        out[...] = total * factor


def grad(scalars, keys, factor, first, second, sums, made):
    rows, width = first.shape[1], made[0][1].shape[1]
    made = [in_vmem(array) for part in made for array in part]
    more = () if keys else (jax.ShapeDtypeStruct((8, 2 * rows), F32),) * 2
    return pl.pallas_call(
        functools.partial(grad_kernel, keys, factor),
        out_shape=(kept((rows, width), F32),) * 2 + more,
        in_specs=[SCALAR] + [WHOLE] * (2 + len(sums) + len(made)),
        out_specs=(WHOLE,) * (2 + len(more)),
        scratch_shapes=[pltpu.VMEM((2 * rows, 8 * rows), jnp.bfloat16)],
        compiler_params=pltpu.CompilerParams(vmem_limit_bytes=VMEM_LIMIT),
        cost_estimate=pl.CostEstimate(
            flops=32 * rows * rows * width,
            bytes_accessed=8 * rows * width * 2 + 64 * rows * rows + rows * width * 8,
            transcendentals=32 * rows * rows,
        ),
    )(scalars, first, second, *sums, *made)


def add_kernel(own, received, out, total, sems):
    parts = sems.shape[0]
    step = own.shape[0] // parts
    writes = []
    for i in range(parts):
        here = pl.ds(i * step, step)
        total[here, :] = own[here, :] + received[here, :]
        writes.append(pltpu.make_async_copy(total.at[here], out.at[here], sems.at[i]))
        writes[-1].start()
    for write in writes:
        write.wait()


def add(own, received):
    return pl.pallas_call(
        add_kernel,
        out_shape=jax.ShapeDtypeStruct(own.shape, F32),
        in_specs=[WHOLE] * 2,
        out_specs=ANYWHERE,
        scratch_shapes=[pltpu.VMEM(own.shape, F32), pltpu.SemaphoreType.DMA((4,))],
        compiler_params=pltpu.CompilerParams(vmem_limit_bytes=VMEM_LIMIT),
        cost_estimate=pl.CostEstimate(flops=own.size, bytes_accessed=12 * own.size, transcendentals=0),
    )(in_vmem(own), in_vmem(received))


def local(query_rows, key_rows, partner):
    rows, features = query_rows.shape
    factor = float(features) ** (-0.5)
    block = lax.axis_index("blk")
    place = lax.axis_index("pb")
    even = block % 2 == 0
    starts = [(place ^ other) * rows for other in (0, 2, 1, 3)]
    scalars = jnp.stack([even.astype(jnp.int32), *starts])
    pick = functools.partial(choose, scalars)

    across = lambda a: shift(a, PART_AXIS, lambda i: i ^ 2)
    core = lambda a: shift(a, PART_AXIS, lambda i: i ^ 1)
    corner = lambda a: shift(a, PART_AXIS, lambda i: i ^ 3)
    beside = lambda a, among=None: shift(a, BLOCK_AXIS, lambda i: i ^ 1, among)
    ahead = lambda a: shift(a, BLOCK_AXIS, lambda i: i + 2)
    back = lambda a: shift(a, BLOCK_AXIS, lambda i: i - 2)
    apart = lambda a: shift(a, BLOCK_AXIS, lambda i: i + 2 if i % 2 == 0 else i - 2)

    k0, q0 = key_rows, query_rows
    kz, partner_core, partner_across = ahead(k0), core(partner), across(partner)
    kx = across(after(k0, partner_across))
    y1_odd = beside(after(k0, partner_core), lambda i: i % 2 == 0)
    y1_even = beside(after(q0, partner_core), lambda i: i % 2 == 1)
    ks, qs = core(k0), core(q0)

    qx = across(after(q0, kx))
    kzy = beside(after(kz, y1_odd, y1_even))
    qz = back(after(q0, kz))

    kzx = across(after(kz, qx))
    qzy = beside(after(qz, kzy))
    m1 = apart(after(pick(kzy, qx), qz))

    kd0 = pick(m1, y1_odd)
    kzxy = beside(after(kzx, qzy))
    m2 = back(after(pick(qx, qzy), m1))
    qd0, qzx = pick(y1_even, m2), pick(m2, m1)

    mine = (q0, qs)
    *k_made_0, info = score(scalars, mine, (k0, kx, kz, kzy), 0, True, factor, (partner, partner_core))
    *q_made_0, tick = score(scalars, (k0, ks), (q0, qx, qz, qzy), 0, False, factor, (partner_across,))
    kd1 = across(after(kd0, kzx, info))
    *k_made_1, info, mine = score(scalars, mine, (kzx, kd0), 2, True, factor, (info, tick), keep=True)
    qd1 = across(after(qd0, info))
    *k_made_2, info = score(scalars, mine, (kzxy, kd1), 3, True, factor, (info,))

    next_to = beside(info)
    far = shift(info, BLOCK_AXIS, lambda i: i - 3 if i % 2 == 0 else i + 3)
    both = jnp.concatenate([info, next_to], axis=0)
    chain = small_call(chain_kernel, [(24, rows)], scalars, info, next_to, far, back(both), ahead(both), scalars=1)[0]
    *q_made_1, tick = score(scalars, (after(k0, next_to), ks), (qzx, qd0), 2, False, factor)
    qzxy = beside(after(qzx, next_to))
    chain = after(chain, qd1)
    sums = (chain, across(chain), core(chain), corner(chain))
    *q_made_2, _ = score(scalars, (k0, ks), (qzxy, qd1), 3, False, factor)
    q_own, q_other, col_info, row_info = grad(
        scalars, False, factor, partner, partner_core, sums, (k_made_0, k_made_1, k_made_2)
    )
    k_own, k_other = grad(
        scalars, True, factor, partner, partner_across, (col_info, row_info), (q_made_0, q_made_1, q_made_2)
    )
    loss = small_call(loss_kernel, [(rows,)], scalars, after(partner, k_other), *sums, scalars=1)[0]
    grad_queries = add(q_own, core(q_other))
    grad_keys = add(k_own, core(k_other))
    return (loss, grad_queries, grad_keys)


def solution(mesh):
    return jax.shard_map(
        local,
        mesh=mesh,
        in_specs=(P(("blk", "pb"), None), P(("blk", "pb"), None), P("blk", "pb")),
        out_specs=(P(("blk", "pb")), P(("blk", "pb"), None), P(("blk", "pb"), None)),
        check_vma=False,
    )
```

```python
import functools

import jax
import jax.numpy as jnp
from jax import lax
from jax.experimental import pallas as pl
from jax.experimental.pallas import tpu as pltpu
from jax.sharding import PartitionSpec as P

F32 = jnp.float32
BLOCK_AXIS, PART_AXIS = "blk", "pb"
VMEM_LIMIT = 16 * 1024 * 1024
ANYWHERE = pl.BlockSpec(memory_space=pl.ANY)
WHOLE = pl.BlockSpec(memory_space=pltpu.VMEM)
SCALAR = pl.BlockSpec(memory_space=pltpu.SMEM)
NT = (((1,), (1,)), ((), ()))


def shift(array, axis, move, among=None):
    peers = lax.axis_size(axis)
    pairs = [(i, move(i) % peers) for i in range(peers) if among is None or among(i)]
    return lax.ppermute(array, axis, pairs)


def as_column(row):
    return jnp.broadcast_to(row, (128, row.shape[1])).T[:, 0:1]


def as_row(column):
    return jnp.broadcast_to(column, (column.shape[0], 128)).T[0:1, :]


def log_join(*parts):
    top = functools.reduce(jnp.maximum, parts)
    return top + jnp.log(sum(jnp.exp(part - top) for part in parts))


def fetch(sources, target, sems):
    copies, row = [], 0
    for i, source in enumerate(sources):
        rows = source.shape[0]
        copy = pltpu.make_async_copy(source, target.at[pl.ds(row, rows)], sems.at[i])
        copy.start()
        copies.append(copy)
        row += rows
    return copies


def choose_kernel(flag, first, second, out, sem):
    @pl.when(flag[0] == 1)
    def _():
        pltpu.make_async_copy(first, out, sem).start()

    @pl.when(flag[0] != 1)
    def _():
        pltpu.make_async_copy(second, out, sem).start()

    pltpu.make_async_copy(first, out, sem).wait()


def choose(flag, first, second):
    return pl.pallas_call(
        choose_kernel,
        out_shape=jax.ShapeDtypeStruct(first.shape, first.dtype),
        in_specs=[SCALAR, ANYWHERE, ANYWHERE],
        out_specs=WHOLE,
        scratch_shapes=[pltpu.SemaphoreType.DMA],
        compiler_params=pltpu.CompilerParams(vmem_limit_bytes=VMEM_LIMIT),
        cost_estimate=pl.CostEstimate(flops=0, bytes_accessed=2 * first.size * 2, transcendentals=0),
    )(flag, first, second)


def after(value, *landed):
    return lax.optimization_barrier((value, landed))[0]


def kept(shape, dtype):
    return pltpu.VMEM(shape, dtype)


def in_vmem(array):
    return pltpu.with_memory_space_constraint(array, pltpu.VMEM)


def ids(scalars, which, rows):
    return scalars[which] + lax.broadcasted_iota(jnp.int32, (1, rows), 1)


def side_by_side(first, second):
    return jnp.concatenate([first, second], axis=1)


def score_kernel(count, given, start, stats, factor, scalars, *refs):
    refs = list(refs)
    mine = refs.pop(0) if given else (refs.pop(0), refs.pop(0))
    shards = [refs.pop(0) for _ in range(count)]
    if given:
        *side, out, right, info, sems = refs
        left = mine
    else:
        *side, out, right, info, left, sems = refs
    copies = fetch(shards, right, sems.at[pl.ds(2, count)])
    if not given:
        for copy in fetch(mine, left, sems):
            copy.wait()
    pair = left.shape[0]
    rows = pair // 2
    lhs = left[...]
    row_parts = []
    if not stats:
        info[...] = jnp.zeros(info.shape, F32)
    elif start:
        info[...] = side[0][...]
    waiting = copies
    ends = [sum(shard.shape[0] for shard in shards[: i + 1]) for i in range(count)]
    for p in range(ends[-1] // pair):
        while waiting and ends[-len(waiting)] - shards[-len(waiting)].shape[0] < (p + 1) * pair:
            waiting.pop(0).wait()
        s = lax.dot_general(
            lhs, right[pl.ds(p * pair, pair), :], NT, preferred_element_type=F32
        ) * factor
        out[:, pl.ds(p * pair, pair)] = s
        if stats:
            col_max = jnp.max(s, axis=0, keepdims=True)
            col = col_max + jnp.log(jnp.sum(jnp.exp(s - col_max), axis=0, keepdims=True))
            row_max = jnp.max(s, axis=1, keepdims=True)
            row_sum = jnp.sum(jnp.exp(s - row_max), axis=1, keepdims=True)
            row_parts.append(row_max + jnp.log(row_sum))
            info[pl.ds(start + p, 1), :] = col
            if start + p == 0:
                chosen = as_column(side_by_side(side[0][...], side[1][...]))
                hit = chosen == side_by_side(ids(scalars, 1, rows), ids(scalars, 2, rows))
                info[pl.ds(5, 1), :] = as_row(jnp.sum(jnp.where(hit, s, 0.0), axis=1, keepdims=True))
    if stats:
        row = as_row(log_join(*row_parts) if len(row_parts) > 1 else row_parts[0])
        if start:
            row = log_join(row, side[0][pl.ds(4, 1), :])
        else:
            info[pl.ds(2, 2), :] = jnp.zeros((2, pair), F32)
            info[pl.ds(6, 2), :] = jnp.zeros((2, pair), F32)
        info[pl.ds(4, 1), :] = row


def score(scalars, mine, shards, start, stats, factor, side=(), keep=False):
    given = not isinstance(mine, tuple)
    width = shards[0].shape[1]
    rows = mine.shape[0] // 2 if given else mine[0].shape[0]
    tokens = sum(shard.shape[0] for shard in shards) // rows
    info = (8, 2 * rows) if stats else (8, 128)
    shapes = [
        kept((2 * rows, tokens * rows), F32),
        kept((tokens * rows, width), jnp.bfloat16),
        jax.ShapeDtypeStruct(info, F32),
    ]
    left = (2 * rows, width)
    if keep:
        shapes.append(kept(left, jnp.bfloat16))
    lhs, lhs_specs = ([in_vmem(mine)], [WHOLE]) if given else (mine, [ANYWHERE] * 2)
    return pl.pallas_call(
        functools.partial(score_kernel, len(shards), given, start, stats, factor),
        out_shape=tuple(shapes),
        in_specs=[SCALAR] + lhs_specs + [ANYWHERE] * len(shards) + [WHOLE] * len(side),
        out_specs=(WHOLE,) * len(shapes),
        scratch_shapes=([] if given or keep else [pltpu.VMEM(left, jnp.bfloat16)])
        + [pltpu.SemaphoreType.DMA((2 + len(shards),))],
        compiler_params=pltpu.CompilerParams(vmem_limit_bytes=VMEM_LIMIT),
        cost_estimate=pl.CostEstimate(
            flops=4 * rows * rows * tokens * width,
            bytes_accessed=(tokens + 2) * rows * width * 2 + 8 * rows * rows * tokens,
            transcendentals=4 * rows * rows * tokens if stats else 0,
        ),
    )(scalars, *lhs, *shards, *side)


def halves(line):
    n = line.shape[1] // 2
    return line[:, :n], line[:, n:]


def by_shard(lines):
    p = [halves(line) for line in lines]
    return [p[0][0], p[0][1], p[1][0], p[2][0], p[1][1], p[3][0], p[2][1], p[3][1]]


def chain_kernel(scalars, own, beside, far, ahead, behind, out):
    even = scalars[0] == 1
    size = own.shape[0]

    def pick(first, second):
        return jnp.where(even, first, second)

    def line(d, i):
        one = lambda ref, at=0: ref[pl.ds(at + i, 1), :]
        if d == 0:
            return one(own)
        if d in (2, -2):
            return one(ahead if d == 2 else behind)
        if d == 1:
            return pick(one(beside), one(ahead, size))
        if d == -1:
            return pick(one(behind, size), one(beside))
        if d == 3:
            return pick(one(ahead, size), one(far))
        return pick(one(far), one(behind, size))

    shards = {d: by_shard([line(d, i) for i in range(4)]) for d in range(-3, 4)}

    def total(step, half):
        parts = []
        for other in range(4):
            d = other - step
            if other % 2 == 0:
                parts.append(shards[d][other + half])
            else:
                c, e = shards[d][4 + half], shards[d][6 + half]
                c_first = (other == 1) == (d % 2 == 0)
                parts.append(pick(c, e) if c_first else pick(e, c))
        return log_join(*parts)

    sums = [[total(step, half) for half in range(2)] for step in range(4)]
    for half in range(2):
        out[pl.ds(half, 1), :] = sums[0][half]
        out[pl.ds(2 + half, 1), :] = sums[2][half]
        out[pl.ds(4 + half, 1), :] = pick(sums[1][half], sums[3][half])
        out[pl.ds(6 + half, 1), :] = pick(sums[3][half], sums[1][half])
    row = {d: halves(line(d, 4)) for d in range(4)}
    for half in range(2):
        at = 8 + 4 * half
        out[pl.ds(at, 1), :] = row[0][half]
        out[pl.ds(at + 1, 1), :] = row[2][half]
        out[pl.ds(at + 2, 1), :] = pick(row[3][half], row[1][half])
        out[pl.ds(at + 3, 1), :] = pick(row[1][half], row[3][half])
    positive = halves(line(0, 5))
    out[pl.ds(16, 1), :] = positive[0]
    out[pl.ds(17, 1), :] = positive[1]
    out[pl.ds(18, 6), :] = jnp.zeros((6, out.shape[1]), F32)


def block_sums(own, across, core, corner):
    line = lambda ref, i: ref[pl.ds(i, 1), :]
    col = [[log_join(line(own, 2 * i + h), line(across, 2 * i + 1 - h)) for h in range(2)] for i in range(4)]
    core_col = [log_join(line(core, h), line(corner, 1 - h)) for h in range(2)]
    row = [
        [log_join(line(own, 8 + i), line(core, 12 + i)), log_join(line(across, 8 + i), line(corner, 12 + i))]
        for i in range(4)
    ]
    core_row = log_join(line(own, 12), line(core, 8))
    return col, core_col, row, core_row


def fill_info(sums, col_out, row_out):
    col, core_col, row, core_row = sums
    zeros = jnp.zeros((3, col_out.shape[1]), F32)
    for out, part, more in ((col_out, col, core_col[0]), (row_out, row, core_row)):
        a, b, c, d = part
        out[pl.ds(0, 1), :] = side_by_side(a[0], a[1])
        out[pl.ds(1, 1), :] = side_by_side(b[0], c[0])
        out[pl.ds(2, 1), :] = side_by_side(b[1], d[0])
        out[pl.ds(3, 1), :] = side_by_side(c[1], d[1])
        out[pl.ds(4, 1), :] = side_by_side(a[0], more)
        out[pl.ds(5, 3), :] = zeros


def loss_kernel(scalars, partner, own, across, core, corner, out):
    col, core_col, row, _ = block_sums(own, across, core, corner)
    chosen = as_column(partner[...])
    found = jnp.zeros(chosen.shape, F32)
    for i, value in enumerate((col[0][0], col[0][1], core_col[0], core_col[1])):
        hit = chosen == ids(scalars, i + 1, value.shape[1])
        found = found + jnp.sum(jnp.where(hit, value, 0.0), axis=1, keepdims=True)
    score = own[pl.ds(16, 1), :] + core[pl.ds(17, 1), :]
    out[...] = (0.5 * row[0][0] + 0.5 * as_row(found) - score)[0]


def small_call(kernel, shapes, *args, scalars=0):
    return pl.pallas_call(
        kernel,
        out_shape=tuple(jax.ShapeDtypeStruct(s, F32) for s in shapes),
        in_specs=[SCALAR] * scalars + [WHOLE] * (len(args) - scalars),
        out_specs=(WHOLE,) * len(shapes),
        compiler_params=pltpu.CompilerParams(vmem_limit_bytes=VMEM_LIMIT),
        cost_estimate=pl.CostEstimate(flops=100000, bytes_accessed=400000, transcendentals=20000),
    )(*args)


def grad_kernel(keys, factor, scalars, first, second, *refs):
    rows = first.shape[1]
    pair = 2 * rows
    if keys:
        row_info, col_info, *made, own_out, other_out, weights = refs
    else:
        *made, own_out, other_out, col_info, row_info, weights = refs[4:]
        fill_info(block_sums(*refs[:4]), col_info, row_info)
    made = list(zip(made[::2], made[1::2]))
    row = as_column(row_info[pl.ds(4, 1), :])
    partners = side_by_side(first[...], second[...])
    across = side_by_side(ids(scalars, 1, rows), ids(scalars, 2, rows))
    if keys:
        row_ids, col_ids = as_column(side_by_side(ids(scalars, 1, rows), ids(scalars, 3, rows))), partners
    else:
        row_ids, col_ids = as_column(partners), across

    def weigh(p, group, s):
        here = slice(group * rows, (group + 1) * rows)
        w = 0.5 * jnp.exp(s - row[here]) + 0.5 * jnp.exp(s - col_info[pl.ds(p, 1), :])
        if p == 0:
            w = w - jnp.where(row_ids[here] == col_ids, 1.0, 0.0)
        weights[pl.ds(group * rows, rows), pl.ds(p * pair, pair)] = w.astype(jnp.bfloat16)

    p = 0
    for scores, _ in made:
        for at in range(0, scores.shape[1], pair):
            for group in (1, 0):
                weigh(p, group, scores[pl.ds(group * rows, rows), pl.ds(at, pair)])
            p += 1
    for group, out in ((1, other_out), (0, own_out)):
        there = pl.ds(group * rows, rows)
        total, at = None, 0
        for _, held in made:
            span = held.shape[0]
            part = jnp.dot(weights[there, pl.ds(at, span)], held[...], preferred_element_type=F32)
            total = part if total is None else total + part
            at += span
        out[...] = total * factor


def grad(scalars, keys, factor, first, second, sums, made):
    rows, width = first.shape[1], made[0][1].shape[1]
    made = [in_vmem(array) for part in made for array in part]
    more = () if keys else (jax.ShapeDtypeStruct((8, 2 * rows), F32),) * 2
    return pl.pallas_call(
        functools.partial(grad_kernel, keys, factor),
        out_shape=(kept((rows, width), F32),) * 2 + more,
        in_specs=[SCALAR] + [WHOLE] * (2 + len(sums) + len(made)),
        out_specs=(WHOLE,) * (2 + len(more)),
        scratch_shapes=[pltpu.VMEM((2 * rows, 8 * rows), jnp.bfloat16)],
        compiler_params=pltpu.CompilerParams(vmem_limit_bytes=VMEM_LIMIT),
        cost_estimate=pl.CostEstimate(
            flops=32 * rows * rows * width,
            bytes_accessed=8 * rows * width * 2 + 64 * rows * rows + rows * width * 8,
            transcendentals=32 * rows * rows,
        ),
    )(scalars, first, second, *sums, *made)


def add_kernel(own, received, out, total, sems):
    parts = sems.shape[0]
    step = own.shape[0] // parts
    writes = []
    for i in range(parts):
        here = pl.ds(i * step, step)
        total[here, :] = own[here, :] + received[here, :]
        writes.append(pltpu.make_async_copy(total.at[here], out.at[here], sems.at[i]))
        writes[-1].start()
    for write in writes:
        write.wait()


def add(own, received):
    return pl.pallas_call(
        add_kernel,
        out_shape=jax.ShapeDtypeStruct(own.shape, F32),
        in_specs=[WHOLE] * 2,
        out_specs=ANYWHERE,
        scratch_shapes=[pltpu.VMEM(own.shape, F32), pltpu.SemaphoreType.DMA((4,))],
        compiler_params=pltpu.CompilerParams(vmem_limit_bytes=VMEM_LIMIT),
        cost_estimate=pl.CostEstimate(flops=own.size, bytes_accessed=12 * own.size, transcendentals=0),
    )(in_vmem(own), in_vmem(received))


def local(query_rows, key_rows, partner):
    rows, features = query_rows.shape
    factor = float(features) ** (-0.5)
    block = lax.axis_index("blk")
    place = lax.axis_index("pb")
    even = block % 2 == 0
    starts = [(place ^ other) * rows for other in (0, 2, 1, 3)]
    scalars = jnp.stack([even.astype(jnp.int32), *starts])
    pick = functools.partial(choose, scalars)

    across = lambda a: shift(a, PART_AXIS, lambda i: i ^ 2)
    core = lambda a: shift(a, PART_AXIS, lambda i: i ^ 1)
    corner = lambda a: shift(a, PART_AXIS, lambda i: i ^ 3)
    beside = lambda a, among=None: shift(a, BLOCK_AXIS, lambda i: i ^ 1, among)
    ahead = lambda a: shift(a, BLOCK_AXIS, lambda i: i + 2)
    back = lambda a: shift(a, BLOCK_AXIS, lambda i: i - 2)
    apart = lambda a: shift(a, BLOCK_AXIS, lambda i: i + 2 if i % 2 == 0 else i - 2)

    k0, q0 = key_rows, query_rows
    kz, partner_core, partner_across = ahead(k0), core(partner), across(partner)
    kx = across(after(k0, partner_across))
    y1_odd = beside(after(k0, partner_core), lambda i: i % 2 == 0)
    y1_even = beside(after(q0, partner_core), lambda i: i % 2 == 1)
    ks, qs = core(k0), core(q0)

    qx = across(after(q0, kx))
    kzy = beside(after(kz, y1_odd, y1_even))
    qz = back(after(q0, kz))

    kzx = across(after(kz, qx))
    qzy = beside(qz)
    m1 = apart(after(pick(kzy, qx), qz))

    kd0 = pick(m1, y1_odd)
    kzxy = beside(after(kzx, qzy))
    m2 = back(after(pick(qx, qzy), m1))
    qd0, qzx = pick(y1_even, m2), pick(m2, m1)

    mine = (q0, qs)
    *k_made_0, info = score(scalars, mine, (k0, kx, kz, kzy), 0, True, factor, (partner, partner_core))
    *q_made_0, tick = score(scalars, (k0, ks), (q0, qx, qz, qzy), 0, False, factor, (partner_across,))
    kd1 = across(after(kd0, kzx, info))
    *k_made_1, info, mine = score(scalars, mine, (kzx, kd0), 2, True, factor, (info, tick), keep=True)
    qd1 = across(after(qd0, info))
    *k_made_2, info = score(scalars, mine, (kzxy, kd1), 3, True, factor, (info,))

    next_to = beside(info)
    far = shift(info, BLOCK_AXIS, lambda i: i - 3 if i % 2 == 0 else i + 3)
    both = jnp.concatenate([info, next_to], axis=0)
    chain = small_call(chain_kernel, [(24, rows)], scalars, info, next_to, far, back(both), ahead(both), scalars=1)[0]
    *q_made_1, tick = score(scalars, (after(k0, next_to), ks), (qzx, qd0), 2, False, factor)
    qzxy = beside(after(qzx, next_to))
    chain = after(chain, qd1)
    sums = (chain, across(chain), core(chain), corner(chain))
    *q_made_2, _ = score(scalars, (k0, ks), (qzxy, qd1), 3, False, factor)
    q_own, q_other, col_info, row_info = grad(
        scalars, False, factor, partner, partner_core, sums, (k_made_0, k_made_1, k_made_2)
    )
    k_own, k_other = grad(
        scalars, True, factor, partner, partner_across, (col_info, row_info), (q_made_0, q_made_1, q_made_2)
    )
    loss = small_call(loss_kernel, [(rows,)], scalars, after(partner, q_other), *sums, scalars=1)[0]
    grad_queries = add(q_own, core(q_other))
    grad_keys = add(k_own, core(k_other))
    return (loss, grad_queries, grad_keys)


def solution(mesh):
    return jax.shard_map(
        local,
        mesh=mesh,
        in_specs=(P(("blk", "pb"), None), P(("blk", "pb"), None), P("blk", "pb")),
        out_specs=(P(("blk", "pb")), P(("blk", "pb"), None), P(("blk", "pb"), None)),
        check_vma=False,
    )
```

```python
import functools

import jax
import jax.numpy as jnp
from jax import lax
from jax.experimental import pallas as pl
from jax.experimental.pallas import tpu as pltpu
from jax.sharding import PartitionSpec as P

F32 = jnp.float32
BLOCK_AXIS, PART_AXIS = "blk", "pb"
VMEM_LIMIT = 16 * 1024 * 1024
ANYWHERE = pl.BlockSpec(memory_space=pl.ANY)
WHOLE = pl.BlockSpec(memory_space=pltpu.VMEM)
SCALAR = pl.BlockSpec(memory_space=pltpu.SMEM)
NT = (((1,), (1,)), ((), ()))


def shift(array, axis, move, among=None):
    peers = lax.axis_size(axis)
    pairs = [(i, move(i) % peers) for i in range(peers) if among is None or among(i)]
    return lax.ppermute(array, axis, pairs)


def as_column(row):
    return jnp.broadcast_to(row, (128, row.shape[1])).T[:, 0:1]


def as_row(column):
    return jnp.broadcast_to(column, (column.shape[0], 128)).T[0:1, :]


def log_join(*parts):
    top = functools.reduce(jnp.maximum, parts)
    return top + jnp.log(sum(jnp.exp(part - top) for part in parts))


def fetch(sources, target, sems):
    copies, row = [], 0
    for i, source in enumerate(sources):
        rows = source.shape[0]
        copy = pltpu.make_async_copy(source, target.at[pl.ds(row, rows)], sems.at[i])
        copy.start()
        copies.append(copy)
        row += rows
    return copies


def choose_kernel(flag, first, second, out, sem):
    @pl.when(flag[0] == 1)
    def _():
        pltpu.make_async_copy(first, out, sem).start()

    @pl.when(flag[0] != 1)
    def _():
        pltpu.make_async_copy(second, out, sem).start()

    pltpu.make_async_copy(first, out, sem).wait()


def choose(flag, first, second):
    return pl.pallas_call(
        choose_kernel,
        out_shape=jax.ShapeDtypeStruct(first.shape, first.dtype),
        in_specs=[SCALAR, ANYWHERE, ANYWHERE],
        out_specs=WHOLE,
        scratch_shapes=[pltpu.SemaphoreType.DMA],
        compiler_params=pltpu.CompilerParams(vmem_limit_bytes=VMEM_LIMIT),
        cost_estimate=pl.CostEstimate(flops=0, bytes_accessed=2 * first.size * 2, transcendentals=0),
    )(flag, first, second)


def after(value, *landed):
    return lax.optimization_barrier((value, landed))[0]


def kept(shape, dtype):
    return pltpu.VMEM(shape, dtype)


def in_vmem(array):
    return pltpu.with_memory_space_constraint(array, pltpu.VMEM)


def ids(scalars, which, rows):
    return scalars[which] + lax.broadcasted_iota(jnp.int32, (1, rows), 1)


def side_by_side(first, second):
    return jnp.concatenate([first, second], axis=1)


def score_kernel(count, given, start, stats, factor, scalars, *refs):
    refs = list(refs)
    mine = refs.pop(0) if given else (refs.pop(0), refs.pop(0))
    shards = [refs.pop(0) for _ in range(count)]
    if given:
        *side, out, right, info, sems = refs
        left = mine
    else:
        *side, out, right, info, left, sems = refs
    copies = fetch(shards, right, sems.at[pl.ds(2, count)])
    if not given:
        for copy in fetch(mine, left, sems):
            copy.wait()
    pair = left.shape[0]
    rows = pair // 2
    lhs = left[...]
    row_parts = []
    if not stats:
        info[...] = jnp.zeros(info.shape, F32)
    elif start:
        info[...] = side[0][...]
    waiting = copies
    ends = [sum(shard.shape[0] for shard in shards[: i + 1]) for i in range(count)]
    for p in range(ends[-1] // pair):
        while waiting and ends[-len(waiting)] - shards[-len(waiting)].shape[0] < (p + 1) * pair:
            waiting.pop(0).wait()
        s = lax.dot_general(
            lhs, right[pl.ds(p * pair, pair), :], NT, preferred_element_type=F32
        ) * factor
        out[:, pl.ds(p * pair, pair)] = s
        if stats:
            col_max = jnp.max(s, axis=0, keepdims=True)
            col = col_max + jnp.log(jnp.sum(jnp.exp(s - col_max), axis=0, keepdims=True))
            row_max = jnp.max(s, axis=1, keepdims=True)
            row_sum = jnp.sum(jnp.exp(s - row_max), axis=1, keepdims=True)
            row_parts.append(row_max + jnp.log(row_sum))
            info[pl.ds(start + p, 1), :] = col
            if start + p == 0:
                chosen = as_column(side_by_side(side[0][...], side[1][...]))
                hit = chosen == side_by_side(ids(scalars, 1, rows), ids(scalars, 2, rows))
                info[pl.ds(5, 1), :] = as_row(jnp.sum(jnp.where(hit, s, 0.0), axis=1, keepdims=True))
    if stats:
        row = as_row(log_join(*row_parts) if len(row_parts) > 1 else row_parts[0])
        if start:
            row = log_join(row, side[0][pl.ds(4, 1), :])
        else:
            info[pl.ds(2, 2), :] = jnp.zeros((2, pair), F32)
            info[pl.ds(6, 2), :] = jnp.zeros((2, pair), F32)
        info[pl.ds(4, 1), :] = row


def score(scalars, mine, shards, start, stats, factor, side=(), keep=False):
    given = not isinstance(mine, tuple)
    width = shards[0].shape[1]
    rows = mine.shape[0] // 2 if given else mine[0].shape[0]
    tokens = sum(shard.shape[0] for shard in shards) // rows
    info = (8, 2 * rows) if stats else (8, 128)
    shapes = [
        kept((2 * rows, tokens * rows), F32),
        kept((tokens * rows, width), jnp.bfloat16),
        jax.ShapeDtypeStruct(info, F32),
    ]
    left = (2 * rows, width)
    if keep:
        shapes.append(kept(left, jnp.bfloat16))
    lhs, lhs_specs = ([in_vmem(mine)], [WHOLE]) if given else (mine, [ANYWHERE] * 2)
    return pl.pallas_call(
        functools.partial(score_kernel, len(shards), given, start, stats, factor),
        out_shape=tuple(shapes),
        in_specs=[SCALAR] + lhs_specs + [ANYWHERE] * len(shards) + [WHOLE] * len(side),
        out_specs=(WHOLE,) * len(shapes),
        scratch_shapes=([] if given or keep else [pltpu.VMEM(left, jnp.bfloat16)])
        + [pltpu.SemaphoreType.DMA((2 + len(shards),))],
        compiler_params=pltpu.CompilerParams(vmem_limit_bytes=VMEM_LIMIT),
        cost_estimate=pl.CostEstimate(
            flops=4 * rows * rows * tokens * width,
            bytes_accessed=(tokens + 2) * rows * width * 2 + 8 * rows * rows * tokens,
            transcendentals=4 * rows * rows * tokens if stats else 0,
        ),
    )(scalars, *lhs, *shards, *side)


def halves(line):
    n = line.shape[1] // 2
    return line[:, :n], line[:, n:]


def by_shard(lines):
    p = [halves(line) for line in lines]
    return [p[0][0], p[0][1], p[1][0], p[2][0], p[1][1], p[3][0], p[2][1], p[3][1]]


def chain_kernel(scalars, own, beside, far, ahead, behind, out):
    even = scalars[0] == 1
    size = own.shape[0]

    def pick(first, second):
        return jnp.where(even, first, second)

    def line(d, i):
        one = lambda ref, at=0: ref[pl.ds(at + i, 1), :]
        if d == 0:
            return one(own)
        if d in (2, -2):
            return one(ahead if d == 2 else behind)
        if d == 1:
            return pick(one(beside), one(ahead, size))
        if d == -1:
            return pick(one(behind, size), one(beside))
        if d == 3:
            return pick(one(ahead, size), one(far))
        return pick(one(far), one(behind, size))

    shards = {d: by_shard([line(d, i) for i in range(4)]) for d in range(-3, 4)}

    def total(step, half):
        parts = []
        for other in range(4):
            d = other - step
            if other % 2 == 0:
                parts.append(shards[d][other + half])
            else:
                c, e = shards[d][4 + half], shards[d][6 + half]
                c_first = (other == 1) == (d % 2 == 0)
                parts.append(pick(c, e) if c_first else pick(e, c))
        return log_join(*parts)

    sums = [[total(step, half) for half in range(2)] for step in range(4)]
    for half in range(2):
        out[pl.ds(half, 1), :] = sums[0][half]
        out[pl.ds(2 + half, 1), :] = sums[2][half]
        out[pl.ds(4 + half, 1), :] = pick(sums[1][half], sums[3][half])
        out[pl.ds(6 + half, 1), :] = pick(sums[3][half], sums[1][half])
    row = {d: halves(line(d, 4)) for d in range(4)}
    for half in range(2):
        at = 8 + 4 * half
        out[pl.ds(at, 1), :] = row[0][half]
        out[pl.ds(at + 1, 1), :] = row[2][half]
        out[pl.ds(at + 2, 1), :] = pick(row[3][half], row[1][half])
        out[pl.ds(at + 3, 1), :] = pick(row[1][half], row[3][half])
    positive = halves(line(0, 5))
    out[pl.ds(16, 1), :] = positive[0]
    out[pl.ds(17, 1), :] = positive[1]
    out[pl.ds(18, 6), :] = jnp.zeros((6, out.shape[1]), F32)


def block_sums(own, across, core, corner):
    line = lambda ref, i: ref[pl.ds(i, 1), :]
    col = [[log_join(line(own, 2 * i + h), line(across, 2 * i + 1 - h)) for h in range(2)] for i in range(4)]
    core_col = [log_join(line(core, h), line(corner, 1 - h)) for h in range(2)]
    row = [
        [log_join(line(own, 8 + i), line(core, 12 + i)), log_join(line(across, 8 + i), line(corner, 12 + i))]
        for i in range(4)
    ]
    core_row = log_join(line(own, 12), line(core, 8))
    return col, core_col, row, core_row


def fill_info(sums, score, col_out, row_out):
    col, core_col, row, core_row = sums
    none = jnp.zeros(score.shape, F32)
    zeros = jnp.zeros((2, col_out.shape[1]), F32)
    for out, part, more, fifth in (
        (col_out, col, core_col[0], side_by_side(core_col[1], score)),
        (row_out, row, core_row, side_by_side(none, none)),
    ):
        a, b, c, d = part
        out[pl.ds(0, 1), :] = side_by_side(a[0], a[1])
        out[pl.ds(1, 1), :] = side_by_side(b[0], c[0])
        out[pl.ds(2, 1), :] = side_by_side(b[1], d[0])
        out[pl.ds(3, 1), :] = side_by_side(c[1], d[1])
        out[pl.ds(4, 1), :] = side_by_side(a[0], more)
        out[pl.ds(5, 1), :] = fifth
        out[pl.ds(6, 2), :] = zeros


def loss_kernel(scalars, partner, col_info, row_info, out):
    own, across = halves(col_info[pl.ds(0, 1), :])
    core = halves(col_info[pl.ds(4, 1), :])[1]
    corner, score = halves(col_info[pl.ds(5, 1), :])
    row = halves(row_info[pl.ds(4, 1), :])[0]
    chosen = as_column(partner[...])
    found = jnp.zeros(chosen.shape, F32)
    for i, value in enumerate((own, across, core, corner)):
        hit = chosen == ids(scalars, i + 1, value.shape[1])
        found = found + jnp.sum(jnp.where(hit, value, 0.0), axis=1, keepdims=True)
    out[...] = (0.5 * row + 0.5 * as_row(found) - score)[0]


def small_call(kernel, shapes, *args, scalars=0):
    return pl.pallas_call(
        kernel,
        out_shape=tuple(jax.ShapeDtypeStruct(s, F32) for s in shapes),
        in_specs=[SCALAR] * scalars + [WHOLE] * (len(args) - scalars),
        out_specs=(WHOLE,) * len(shapes),
        compiler_params=pltpu.CompilerParams(vmem_limit_bytes=VMEM_LIMIT),
        cost_estimate=pl.CostEstimate(flops=100000, bytes_accessed=400000, transcendentals=20000),
    )(*args)


def grad_kernel(keys, factor, scalars, first, second, *refs):
    rows = first.shape[1]
    pair = 2 * rows
    if keys:
        row_info, col_info, *made, own_out, other_out, weights = refs
    else:
        *made, own_out, other_out, col_info, row_info, weights = refs[4:]
        score = refs[0][pl.ds(16, 1), :] + refs[2][pl.ds(17, 1), :]
        fill_info(block_sums(*refs[:4]), score, col_info, row_info)
    made = list(zip(made[::2], made[1::2]))
    row = as_column(row_info[pl.ds(4, 1), :])
    partners = side_by_side(first[...], second[...])
    across = side_by_side(ids(scalars, 1, rows), ids(scalars, 2, rows))
    if keys:
        row_ids, col_ids = as_column(side_by_side(ids(scalars, 1, rows), ids(scalars, 3, rows))), partners
    else:
        row_ids, col_ids = as_column(partners), across

    def weigh(p, group, s):
        here = slice(group * rows, (group + 1) * rows)
        w = 0.5 * jnp.exp(s - row[here]) + 0.5 * jnp.exp(s - col_info[pl.ds(p, 1), :])
        if p == 0:
            w = w - jnp.where(row_ids[here] == col_ids, 1.0, 0.0)
        weights[pl.ds(group * rows, rows), pl.ds(p * pair, pair)] = w.astype(jnp.bfloat16)

    p = 0
    for scores, _ in made:
        for at in range(0, scores.shape[1], pair):
            for group in (1, 0):
                weigh(p, group, scores[pl.ds(group * rows, rows), pl.ds(at, pair)])
            p += 1
    for group, out in ((1, other_out), (0, own_out)):
        there = pl.ds(group * rows, rows)
        total, at = None, 0
        for _, held in made:
            span = held.shape[0]
            part = jnp.dot(weights[there, pl.ds(at, span)], held[...], preferred_element_type=F32)
            total = part if total is None else total + part
            at += span
        out[...] = total * factor


def grad(scalars, keys, factor, first, second, sums, made):
    rows, width = first.shape[1], made[0][1].shape[1]
    made = [in_vmem(array) for part in made for array in part]
    more = () if keys else (jax.ShapeDtypeStruct((8, 2 * rows), F32),) * 2
    return pl.pallas_call(
        functools.partial(grad_kernel, keys, factor),
        out_shape=(kept((rows, width), F32),) * 2 + more,
        in_specs=[SCALAR] + [WHOLE] * (2 + len(sums) + len(made)),
        out_specs=(WHOLE,) * (2 + len(more)),
        scratch_shapes=[pltpu.VMEM((2 * rows, 8 * rows), jnp.bfloat16)],
        compiler_params=pltpu.CompilerParams(vmem_limit_bytes=VMEM_LIMIT),
        cost_estimate=pl.CostEstimate(
            flops=32 * rows * rows * width,
            bytes_accessed=8 * rows * width * 2 + 64 * rows * rows + rows * width * 8,
            transcendentals=32 * rows * rows,
        ),
    )(scalars, first, second, *sums, *made)


def add_kernel(own, received, out, total, sems):
    parts = sems.shape[0]
    step = own.shape[0] // parts
    writes = []
    for i in range(parts):
        here = pl.ds(i * step, step)
        total[here, :] = own[here, :] + received[here, :]
        writes.append(pltpu.make_async_copy(total.at[here], out.at[here], sems.at[i]))
        writes[-1].start()
    for write in writes:
        write.wait()


def add(own, received):
    return pl.pallas_call(
        add_kernel,
        out_shape=jax.ShapeDtypeStruct(own.shape, F32),
        in_specs=[WHOLE] * 2,
        out_specs=ANYWHERE,
        scratch_shapes=[pltpu.VMEM(own.shape, F32), pltpu.SemaphoreType.DMA((4,))],
        compiler_params=pltpu.CompilerParams(vmem_limit_bytes=VMEM_LIMIT),
        cost_estimate=pl.CostEstimate(flops=own.size, bytes_accessed=12 * own.size, transcendentals=0),
    )(in_vmem(own), in_vmem(received))


def local(query_rows, key_rows, partner):
    rows, features = query_rows.shape
    factor = float(features) ** (-0.5)
    block = lax.axis_index("blk")
    place = lax.axis_index("pb")
    even = block % 2 == 0
    starts = [(place ^ other) * rows for other in (0, 2, 1, 3)]
    scalars = jnp.stack([even.astype(jnp.int32), *starts])
    pick = functools.partial(choose, scalars)

    across = lambda a: shift(a, PART_AXIS, lambda i: i ^ 2)
    core = lambda a: shift(a, PART_AXIS, lambda i: i ^ 1)
    corner = lambda a: shift(a, PART_AXIS, lambda i: i ^ 3)
    beside = lambda a, among=None: shift(a, BLOCK_AXIS, lambda i: i ^ 1, among)
    ahead = lambda a: shift(a, BLOCK_AXIS, lambda i: i + 2)
    back = lambda a: shift(a, BLOCK_AXIS, lambda i: i - 2)
    apart = lambda a: shift(a, BLOCK_AXIS, lambda i: i + 2 if i % 2 == 0 else i - 2)

    k0, q0 = key_rows, query_rows
    kz, partner_core, partner_across = ahead(k0), core(partner), across(partner)
    kx = across(after(k0, partner_across))
    y1_odd = beside(after(k0, partner_core), lambda i: i % 2 == 0)
    y1_even = beside(after(q0, partner_core), lambda i: i % 2 == 1)
    ks, qs = core(k0), core(q0)

    qx = across(after(q0, kx))
    kzy = beside(after(kz, y1_odd, y1_even))
    qz = back(after(q0, kz))

    kzx = across(after(kz, qx))
    qzy = beside(qz)
    m1 = apart(after(pick(kzy, qx), qz))

    kd0 = pick(m1, y1_odd)
    kzxy = beside(after(kzx, qzy))
    m2 = back(after(pick(qx, qzy), m1))
    qd0, qzx = pick(y1_even, m2), pick(m2, m1)

    mine = (q0, qs)
    *k_made_0, info = score(scalars, mine, (k0, kx, kz, kzy), 0, True, factor, (partner, partner_core))
    *q_made_0, tick = score(scalars, (k0, ks), (q0, qx, qz, qzy), 0, False, factor, (partner_across,))
    kd1 = across(after(kd0, kzx, info))
    *k_made_1, info, mine = score(scalars, mine, (kzx, kd0), 2, True, factor, (info, tick), keep=True)
    qd1 = across(after(qd0, info))
    *k_made_2, info = score(scalars, mine, (kzxy, kd1), 3, True, factor, (info,))

    next_to = beside(info)
    far = shift(info, BLOCK_AXIS, lambda i: i - 3 if i % 2 == 0 else i + 3)
    both = jnp.concatenate([info, next_to], axis=0)
    chain = small_call(chain_kernel, [(24, rows)], scalars, info, next_to, far, back(both), ahead(both), scalars=1)[0]
    *q_made_1, tick = score(scalars, (after(k0, next_to), ks), (qzx, qd0), 2, False, factor)
    qzxy = beside(after(qzx, next_to))
    chain = after(chain, qd1)
    sums = (chain, across(chain), core(chain), corner(chain))
    *q_made_2, _ = score(scalars, (k0, ks), (qzxy, qd1), 3, False, factor)
    q_own, q_other, col_info, row_info = grad(
        scalars, False, factor, partner, partner_core, sums, (k_made_0, k_made_1, k_made_2)
    )
    k_own, k_other = grad(
        scalars, True, factor, partner, partner_across, (col_info, row_info), (q_made_0, q_made_1, q_made_2)
    )
    loss = small_call(loss_kernel, [(rows,)], scalars, partner, col_info, row_info, scalars=1)[0]
    grad_queries = add(q_own, core(q_other))
    grad_keys = add(k_own, core(k_other))
    return (loss, grad_queries, grad_keys)


def solution(mesh):
    return jax.shard_map(
        local,
        mesh=mesh,
        in_specs=(P(("blk", "pb"), None), P(("blk", "pb"), None), P("blk", "pb")),
        out_specs=(P(("blk", "pb")), P(("blk", "pb"), None), P(("blk", "pb"), None)),
        check_vma=False,
    )
```

```python
import functools

import jax
import jax.numpy as jnp
from jax import lax
from jax.experimental import pallas as pl
from jax.experimental.pallas import tpu as pltpu
from jax.sharding import PartitionSpec as P

F32 = jnp.float32
BLOCK_AXIS, PART_AXIS = "blk", "pb"
VMEM_LIMIT = 16 * 1024 * 1024
ANYWHERE = pl.BlockSpec(memory_space=pl.ANY)
WHOLE = pl.BlockSpec(memory_space=pltpu.VMEM)
SCALAR = pl.BlockSpec(memory_space=pltpu.SMEM)
NT = (((1,), (1,)), ((), ()))


def shift(array, axis, move, among=None):
    peers = lax.axis_size(axis)
    pairs = [(i, move(i) % peers) for i in range(peers) if among is None or among(i)]
    return lax.ppermute(array, axis, pairs)


def as_column(row):
    return jnp.broadcast_to(row, (128, row.shape[1])).T[:, 0:1]


def as_row(column):
    return jnp.broadcast_to(column, (column.shape[0], 128)).T[0:1, :]


def log_join(*parts):
    top = functools.reduce(jnp.maximum, parts)
    return top + jnp.log(sum(jnp.exp(part - top) for part in parts))


def fetch(sources, target, sems):
    copies, row = [], 0
    for i, source in enumerate(sources):
        rows = source.shape[0]
        copy = pltpu.make_async_copy(source, target.at[pl.ds(row, rows)], sems.at[i])
        copy.start()
        copies.append(copy)
        row += rows
    return copies


def choose_kernel(flag, first, second, out, sem):
    @pl.when(flag[0] == 1)
    def _():
        pltpu.make_async_copy(first, out, sem).start()

    @pl.when(flag[0] != 1)
    def _():
        pltpu.make_async_copy(second, out, sem).start()

    pltpu.make_async_copy(first, out, sem).wait()


def choose(flag, first, second):
    return pl.pallas_call(
        choose_kernel,
        out_shape=jax.ShapeDtypeStruct(first.shape, first.dtype),
        in_specs=[SCALAR, ANYWHERE, ANYWHERE],
        out_specs=WHOLE,
        scratch_shapes=[pltpu.SemaphoreType.DMA],
        compiler_params=pltpu.CompilerParams(vmem_limit_bytes=VMEM_LIMIT),
        cost_estimate=pl.CostEstimate(flops=0, bytes_accessed=2 * first.size * 2, transcendentals=0),
    )(flag, first, second)


def after(value, *landed):
    return lax.optimization_barrier((value, landed))[0]


def kept(shape, dtype):
    return pltpu.VMEM(shape, dtype)


def in_vmem(array):
    return pltpu.with_memory_space_constraint(array, pltpu.VMEM)


def ids(scalars, which, rows):
    return scalars[which] + lax.broadcasted_iota(jnp.int32, (1, rows), 1)


def side_by_side(first, second):
    return jnp.concatenate([first, second], axis=1)


def score_kernel(count, given, start, stats, factor, scalars, *refs):
    refs = list(refs)
    mine = refs.pop(0) if given else (refs.pop(0), refs.pop(0))
    shards = [refs.pop(0) for _ in range(count)]
    if given:
        *side, out, right, info, sems = refs
        left = mine
    else:
        *side, out, right, info, left, sems = refs
    copies = fetch(shards, right, sems.at[pl.ds(2, count)])
    if not given:
        for copy in fetch(mine, left, sems):
            copy.wait()
    pair = left.shape[0]
    rows = pair // 2
    lhs = left[...]
    row_parts = []
    if not stats:
        info[...] = jnp.zeros(info.shape, F32)
    elif start:
        info[...] = side[0][...]
    waiting = copies
    ends = [sum(shard.shape[0] for shard in shards[: i + 1]) for i in range(count)]
    for p in range(ends[-1] // pair):
        while waiting and ends[-len(waiting)] - shards[-len(waiting)].shape[0] < (p + 1) * pair:
            waiting.pop(0).wait()
        s = lax.dot_general(
            lhs, right[pl.ds(p * pair, pair), :], NT, preferred_element_type=F32
        ) * factor
        out[:, pl.ds(p * pair, pair)] = s
        if stats:
            col_max = jnp.max(s, axis=0, keepdims=True)
            col = col_max + jnp.log(jnp.sum(jnp.exp(s - col_max), axis=0, keepdims=True))
            row_max = jnp.max(s, axis=1, keepdims=True)
            row_sum = jnp.sum(jnp.exp(s - row_max), axis=1, keepdims=True)
            row_parts.append(row_max + jnp.log(row_sum))
            info[pl.ds(start + p, 1), :] = col
            if start + p == 0:
                chosen = as_column(side_by_side(side[0][...], side[1][...]))
                hit = chosen == side_by_side(ids(scalars, 1, rows), ids(scalars, 2, rows))
                info[pl.ds(5, 1), :] = as_row(jnp.sum(jnp.where(hit, s, 0.0), axis=1, keepdims=True))
    if stats:
        row = as_row(log_join(*row_parts) if len(row_parts) > 1 else row_parts[0])
        if start:
            row = log_join(row, side[0][pl.ds(4, 1), :])
        else:
            info[pl.ds(2, 2), :] = jnp.zeros((2, pair), F32)
            info[pl.ds(6, 2), :] = jnp.zeros((2, pair), F32)
        info[pl.ds(4, 1), :] = row


def score(scalars, mine, shards, start, stats, factor, side=(), keep=False):
    given = not isinstance(mine, tuple)
    width = shards[0].shape[1]
    rows = mine.shape[0] // 2 if given else mine[0].shape[0]
    tokens = sum(shard.shape[0] for shard in shards) // rows
    info = (8, 2 * rows) if stats else (8, 128)
    shapes = [
        kept((2 * rows, tokens * rows), F32),
        kept((tokens * rows, width), jnp.bfloat16),
        jax.ShapeDtypeStruct(info, F32),
    ]
    left = (2 * rows, width)
    if keep:
        shapes.append(kept(left, jnp.bfloat16))
    lhs, lhs_specs = ([in_vmem(mine)], [WHOLE]) if given else (mine, [ANYWHERE] * 2)
    return pl.pallas_call(
        functools.partial(score_kernel, len(shards), given, start, stats, factor),
        out_shape=tuple(shapes),
        in_specs=[SCALAR] + lhs_specs + [ANYWHERE] * len(shards) + [WHOLE] * len(side),
        out_specs=(WHOLE,) * len(shapes),
        scratch_shapes=([] if given or keep else [pltpu.VMEM(left, jnp.bfloat16)])
        + [pltpu.SemaphoreType.DMA((2 + len(shards),))],
        compiler_params=pltpu.CompilerParams(vmem_limit_bytes=VMEM_LIMIT),
        cost_estimate=pl.CostEstimate(
            flops=8 * rows * rows * tokens * width,
            bytes_accessed=2 * ((tokens + 2) * rows * width * 2 + 8 * rows * rows * tokens),
            transcendentals=4 * rows * rows * tokens if stats else 0,
        ),
    )(scalars, *lhs, *shards, *side)


def halves(line):
    n = line.shape[1] // 2
    return line[:, :n], line[:, n:]


def by_shard(lines):
    p = [halves(line) for line in lines]
    return [p[0][0], p[0][1], p[1][0], p[2][0], p[1][1], p[3][0], p[2][1], p[3][1]]


def chain_kernel(scalars, own, beside, far, ahead, behind, out):
    even = scalars[0] == 1
    size = own.shape[0]

    def pick(first, second):
        return jnp.where(even, first, second)

    def line(d, i):
        one = lambda ref, at=0: ref[pl.ds(at + i, 1), :]
        if d == 0:
            return one(own)
        if d in (2, -2):
            return one(ahead if d == 2 else behind)
        if d == 1:
            return pick(one(beside), one(ahead, size))
        if d == -1:
            return pick(one(behind, size), one(beside))
        if d == 3:
            return pick(one(ahead, size), one(far))
        return pick(one(far), one(behind, size))

    shards = {d: by_shard([line(d, i) for i in range(4)]) for d in range(-3, 4)}

    def total(step, half):
        parts = []
        for other in range(4):
            d = other - step
            if other % 2 == 0:
                parts.append(shards[d][other + half])
            else:
                c, e = shards[d][4 + half], shards[d][6 + half]
                c_first = (other == 1) == (d % 2 == 0)
                parts.append(pick(c, e) if c_first else pick(e, c))
        return log_join(*parts)

    sums = [[total(step, half) for half in range(2)] for step in range(4)]
    for half in range(2):
        out[pl.ds(half, 1), :] = sums[0][half]
        out[pl.ds(2 + half, 1), :] = sums[2][half]
        out[pl.ds(4 + half, 1), :] = pick(sums[1][half], sums[3][half])
        out[pl.ds(6 + half, 1), :] = pick(sums[3][half], sums[1][half])
    row = {d: halves(line(d, 4)) for d in range(4)}
    for half in range(2):
        at = 8 + 4 * half
        out[pl.ds(at, 1), :] = row[0][half]
        out[pl.ds(at + 1, 1), :] = row[2][half]
        out[pl.ds(at + 2, 1), :] = pick(row[3][half], row[1][half])
        out[pl.ds(at + 3, 1), :] = pick(row[1][half], row[3][half])
    positive = halves(line(0, 5))
    out[pl.ds(16, 1), :] = positive[0]
    out[pl.ds(17, 1), :] = positive[1]
    out[pl.ds(18, 6), :] = jnp.zeros((6, out.shape[1]), F32)


def block_sums(own, across, core, corner):
    line = lambda ref, i: ref[pl.ds(i, 1), :]
    col = [[log_join(line(own, 2 * i + h), line(across, 2 * i + 1 - h)) for h in range(2)] for i in range(4)]
    core_col = [log_join(line(core, h), line(corner, 1 - h)) for h in range(2)]
    row = [
        [log_join(line(own, 8 + i), line(core, 12 + i)), log_join(line(across, 8 + i), line(corner, 12 + i))]
        for i in range(4)
    ]
    core_row = log_join(line(own, 12), line(core, 8))
    return col, core_col, row, core_row


def fill_info(sums, col_out, row_out):
    col, core_col, row, core_row = sums
    zeros = jnp.zeros((3, col_out.shape[1]), F32)
    for out, part, more in ((col_out, col, core_col[0]), (row_out, row, core_row)):
        a, b, c, d = part
        out[pl.ds(0, 1), :] = side_by_side(a[0], a[1])
        out[pl.ds(1, 1), :] = side_by_side(b[0], c[0])
        out[pl.ds(2, 1), :] = side_by_side(b[1], d[0])
        out[pl.ds(3, 1), :] = side_by_side(c[1], d[1])
        out[pl.ds(4, 1), :] = side_by_side(a[0], more)
        out[pl.ds(5, 3), :] = zeros


def loss_kernel(scalars, partner, own, across, core, corner, out):
    col, core_col, row, _ = block_sums(own, across, core, corner)
    chosen = as_column(partner[...])
    found = jnp.zeros(chosen.shape, F32)
    for i, value in enumerate((col[0][0], col[0][1], core_col[0], core_col[1])):
        hit = chosen == ids(scalars, i + 1, value.shape[1])
        found = found + jnp.sum(jnp.where(hit, value, 0.0), axis=1, keepdims=True)
    score = own[pl.ds(16, 1), :] + core[pl.ds(17, 1), :]
    out[...] = (0.5 * row[0][0] + 0.5 * as_row(found) - score)[0]


def small_call(kernel, shapes, *args, scalars=0):
    return pl.pallas_call(
        kernel,
        out_shape=tuple(jax.ShapeDtypeStruct(s, F32) for s in shapes),
        in_specs=[SCALAR] * scalars + [WHOLE] * (len(args) - scalars),
        out_specs=(WHOLE,) * len(shapes),
        compiler_params=pltpu.CompilerParams(vmem_limit_bytes=VMEM_LIMIT),
        cost_estimate=pl.CostEstimate(flops=100000, bytes_accessed=400000, transcendentals=20000),
    )(*args)


def grad_kernel(keys, factor, scalars, first, second, *refs):
    rows = first.shape[1]
    pair = 2 * rows
    if keys:
        row_info, col_info, *made, own_out, other_out, weights = refs
    else:
        *made, own_out, other_out, col_info, row_info, weights = refs[4:]
        fill_info(block_sums(*refs[:4]), col_info, row_info)
    made = list(zip(made[::2], made[1::2]))
    row = as_column(row_info[pl.ds(4, 1), :])
    partners = side_by_side(first[...], second[...])
    across = side_by_side(ids(scalars, 1, rows), ids(scalars, 2, rows))
    if keys:
        row_ids, col_ids = as_column(side_by_side(ids(scalars, 1, rows), ids(scalars, 3, rows))), partners
    else:
        row_ids, col_ids = as_column(partners), across

    def weigh(p, group, s):
        here = slice(group * rows, (group + 1) * rows)
        w = 0.5 * jnp.exp(s - row[here]) + 0.5 * jnp.exp(s - col_info[pl.ds(p, 1), :])
        if p == 0:
            w = w - jnp.where(row_ids[here] == col_ids, 1.0, 0.0)
        weights[pl.ds(group * rows, rows), pl.ds(p * pair, pair)] = w.astype(jnp.bfloat16)

    p = 0
    for scores, _ in made:
        for at in range(0, scores.shape[1], pair):
            for group in (1, 0):
                weigh(p, group, scores[pl.ds(group * rows, rows), pl.ds(at, pair)])
            p += 1
    for group, out in ((1, other_out), (0, own_out)):
        there = pl.ds(group * rows, rows)
        total, at = None, 0
        for _, held in made:
            span = held.shape[0]
            part = jnp.dot(weights[there, pl.ds(at, span)], held[...], preferred_element_type=F32)
            total = part if total is None else total + part
            at += span
        out[...] = total * factor


def grad(scalars, keys, factor, first, second, sums, made):
    rows, width = first.shape[1], made[0][1].shape[1]
    made = [in_vmem(array) for part in made for array in part]
    more = () if keys else (jax.ShapeDtypeStruct((8, 2 * rows), F32),) * 2
    return pl.pallas_call(
        functools.partial(grad_kernel, keys, factor),
        out_shape=(kept((rows, width), F32),) * 2 + more,
        in_specs=[SCALAR] + [WHOLE] * (2 + len(sums) + len(made)),
        out_specs=(WHOLE,) * (2 + len(more)),
        scratch_shapes=[pltpu.VMEM((2 * rows, 8 * rows), jnp.bfloat16)],
        compiler_params=pltpu.CompilerParams(vmem_limit_bytes=VMEM_LIMIT),
        cost_estimate=pl.CostEstimate(
            flops=32 * rows * rows * width,
            bytes_accessed=8 * rows * width * 2 + 64 * rows * rows + rows * width * 8,
            transcendentals=32 * rows * rows,
        ),
    )(scalars, first, second, *sums, *made)


def add_kernel(own, received, out, total, sems):
    parts = sems.shape[0]
    step = own.shape[0] // parts
    writes = []
    for i in range(parts):
        here = pl.ds(i * step, step)
        total[here, :] = own[here, :] + received[here, :]
        writes.append(pltpu.make_async_copy(total.at[here], out.at[here], sems.at[i]))
        writes[-1].start()
    for write in writes:
        write.wait()


def add(own, received):
    return pl.pallas_call(
        add_kernel,
        out_shape=jax.ShapeDtypeStruct(own.shape, F32),
        in_specs=[WHOLE] * 2,
        out_specs=ANYWHERE,
        scratch_shapes=[pltpu.VMEM(own.shape, F32), pltpu.SemaphoreType.DMA((4,))],
        compiler_params=pltpu.CompilerParams(vmem_limit_bytes=VMEM_LIMIT),
        cost_estimate=pl.CostEstimate(flops=own.size, bytes_accessed=12 * own.size, transcendentals=0),
    )(in_vmem(own), in_vmem(received))


def local(query_rows, key_rows, partner):
    rows, features = query_rows.shape
    factor = float(features) ** (-0.5)
    block = lax.axis_index("blk")
    place = lax.axis_index("pb")
    even = block % 2 == 0
    starts = [(place ^ other) * rows for other in (0, 2, 1, 3)]
    scalars = jnp.stack([even.astype(jnp.int32), *starts])
    pick = functools.partial(choose, scalars)

    across = lambda a: shift(a, PART_AXIS, lambda i: i ^ 2)
    core = lambda a: shift(a, PART_AXIS, lambda i: i ^ 1)
    corner = lambda a: shift(a, PART_AXIS, lambda i: i ^ 3)
    beside = lambda a, among=None: shift(a, BLOCK_AXIS, lambda i: i ^ 1, among)
    ahead = lambda a: shift(a, BLOCK_AXIS, lambda i: i + 2)
    back = lambda a: shift(a, BLOCK_AXIS, lambda i: i - 2)
    apart = lambda a: shift(a, BLOCK_AXIS, lambda i: i + 2 if i % 2 == 0 else i - 2)

    k0, q0 = key_rows, query_rows
    kz, partner_core, partner_across = ahead(k0), core(partner), across(partner)
    kx = across(after(k0, partner_across))
    y1_odd = beside(after(k0, partner_core), lambda i: i % 2 == 0)
    y1_even = beside(after(q0, partner_core), lambda i: i % 2 == 1)
    ks, qs = core(k0), core(q0)

    qx = across(after(q0, kx))
    kzy = beside(after(kz, y1_odd, y1_even))
    qz = back(after(q0, kz))

    kzx = across(after(kz, qx))
    qzy = beside(qz)
    m1 = apart(after(pick(kzy, qx), qz))

    kd0 = pick(m1, y1_odd)
    kzxy = beside(after(kzx, qzy))
    m2 = back(after(pick(qx, qzy), m1))
    qd0, qzx = pick(y1_even, m2), pick(m2, m1)

    mine = (q0, qs)
    *k_made_0, info = score(scalars, mine, (k0, kx, kz, kzy), 0, True, factor, (partner, partner_core))
    *q_made_0, tick = score(scalars, (k0, ks), (q0, qx, qz, qzy), 0, False, factor, (partner_across,))
    kd1 = across(after(kd0, kzx, info))
    *k_made_1, info, mine = score(scalars, mine, (kzx, kd0), 2, True, factor, (info, tick), keep=True)
    qd1 = across(after(qd0, info))
    *k_made_2, info = score(scalars, mine, (kzxy, kd1), 3, True, factor, (info,))

    next_to = beside(info)
    far = shift(info, BLOCK_AXIS, lambda i: i - 3 if i % 2 == 0 else i + 3)
    both = jnp.concatenate([info, next_to], axis=0)
    chain = small_call(chain_kernel, [(24, rows)], scalars, info, next_to, far, back(both), ahead(both), scalars=1)[0]
    *q_made_1, tick = score(scalars, (after(k0, next_to), ks), (qzx, qd0), 2, False, factor)
    qzxy = beside(after(qzx, next_to))
    chain = after(chain, qd1)
    sums = (chain, across(chain), core(chain), corner(chain))
    *q_made_2, _ = score(scalars, (k0, ks), (qzxy, qd1), 3, False, factor)
    q_own, q_other, col_info, row_info = grad(
        scalars, False, factor, partner, partner_core, sums, (k_made_0, k_made_1, k_made_2)
    )
    k_own, k_other = grad(
        scalars, True, factor, partner, partner_across, (col_info, row_info), (q_made_0, q_made_1, q_made_2)
    )
    loss = small_call(loss_kernel, [(rows,)], scalars, after(partner, q_other), *sums, scalars=1)[0]
    grad_queries = add(q_own, core(q_other))
    grad_keys = add(k_own, core(k_other))
    return (loss, grad_queries, grad_keys)


def solution(mesh):
    return jax.shard_map(
        local,
        mesh=mesh,
        in_specs=(P(("blk", "pb"), None), P(("blk", "pb"), None), P("blk", "pb")),
        out_specs=(P(("blk", "pb")), P(("blk", "pb"), None), P(("blk", "pb"), None)),
        check_vma=False,
    )
```
